32 devices in a mesh: dp: 8 (over z, x), pair: 4 (over y, core).
Axes of the slice: x: 2, y: 2, z: 4, core: 2. Of those that a mesh axis runs over, the one named last changes fastest.
Arguments:
- table: float32 [16384, 512], P(('dp', 'pair')), may hold values from -6 to 6
- accum: float32 [16384], P(('dp', 'pair')), may hold values from 0.05 to 2
- item_row: int32 [12288], P(('dp', 'pair')), may hold values from 0 to 16383, as said below
- segments: int32 [8, 1536], P('dp'), may hold values from 0 to 1, never falling along the last dimension, each value on 1 to 1344 neighbouring positions
- pairs: int32 [8, 12, 2], P('dp'), may hold values from -1 to 3, as said below
- w_in: bfloat16 [512, 2048], replicated, may hold values from -0.25 to 0.25
- w_out: bfloat16 [512, 512], replicated, may hold values from -0.25 to 0.25
- out_grad: bfloat16 [12288, 512], P(('dp', 'pair')), may hold values from -6 to 6
Outputs:
- layer_out: bfloat16 [12288, 512], P(('dp', 'pair'))
- table_new: float32 [16384, 512], P(('dp', 'pair'))
- accum_new: float32 [16384], P(('dp', 'pair'))
- grad_in: float32 [512, 2048], P(('dp', 'pair'))
- grad_out: float32 [512, 512], P(('dp', 'pair'))
The draws below stay inside these ranges and needn't reach their ends.
Inputs may be any that keep to these rules, and one draw needn't show every extreme that they name: Row r is held by device r // 512 at slot r % 512. The 384 actions of one device (aligned blocks of item_row) name rows of any one device at most 24 times, repeats counted; in every draw one device receives exactly 24 from every device. Row g lists causal block pairs (query block, key block) of the group, key block at most query block, each at most once; every diagonal pair and every pair with key block 0 is listed, the other causal pairs some of them; slots s * 3 to s * 3 + 2 belong to index s of pair; unused slots hold (-1, -1). `segments`: actions with equal ids in a group belong to one history.
All inputs are finite; a program needn't handle non-finite values.
Results may differ from the reference program's by a relative error of at most 0.0025.
The reference program's roundings to bfloat16 on the way count: a program that leaves them out, or rounds other values in their place, can miss the bound.
Values may be sent and summed in bfloat16 or wider, within the bound.
No kernel may reach another device: no remote copies, remote signals or barrier semaphores. Data moves between devices by JAX's collectives and lax.ppermute only.
A program may use at most 192 MiB of HBM per device.

```python
import math
import jax
import jax.numpy as jnp
import numpy as np
from jax import lax

D = 512
HEADS = 8
DH = 64
TOK_DEV = 384
ROWS_DEV = 512
SHARDS = 32
SPAN = 4
GROUPS = 8
GROUP_ROWS = 1536
PCAP = 3
TOKENS = 12288
ROWS = 16384


def draw_item_row(key, part):
    per_owner = TOK_DEV // SHARDS
    bound_rows = 2 * per_owner
    halves = SHARDS // 2
    key_list = jax.random.split(key, 6)
    chosen = jax.random.randint(key_list[0], (), 0, halves)
    full_side = jax.random.randint(key_list[1], (), 0, 2)
    first_count = jax.random.randint(key_list[2], (SHARDS, halves), 1, bound_rows)
    flipped = jax.random.randint(key_list[3], (SHARDS, halves), 0, 2)
    first_count = jnp.where(flipped == 1, bound_rows - first_count, first_count)
    full_first = jnp.where(full_side == 0, bound_rows, 0)
    first_count = jnp.where(jnp.arange(halves)[None, :] == chosen, full_first, first_count)
    counts = jnp.stack([first_count, bound_rows - first_count], axis=2).reshape(SHARDS, SHARDS)
    bucket_ends = jnp.cumsum(counts, axis=1)
    places = jnp.arange(TOK_DEV)
    owners = jnp.sum((bucket_ends[:, None, :] <= places[None, :, None]).astype(jnp.int32), axis=2)
    row_keys = jax.random.split(key_list[4], SHARDS)
    owners = jax.vmap(lambda subkey, owner_row: jax.random.permutation(subkey, owner_row))(row_keys, owners)
    row_slots = jax.random.randint(key_list[5], (SHARDS, TOK_DEV), 0, ROWS_DEV)
    return (owners * ROWS_DEV + row_slots).reshape(TOKENS).astype(jnp.int32)


def draw_pairs(key, part):
    pair_total = SPAN * (SPAN + 1) // 2
    order_index = jnp.arange(SPAN * SPAN)
    query_block = order_index // SPAN
    key_block = order_index % SPAN
    priority = jnp.where(query_block >= key_block, 0, 1) * (SPAN * SPAN) + order_index
    ordering = jnp.argsort(priority)[:pair_total]
    causal_query = query_block[ordering]
    causal_key = key_block[ordering]
    always = (causal_query == causal_key) | (causal_key == 0)

    def one_group(group_key):
        key_list = jax.random.split(group_key, 3)
        shuffled = jax.random.permutation(key_list[0], pair_total)
        coin = jax.random.randint(key_list[1], (pair_total,), 0, 2)
        keep = (always | (coin == 1))[shuffled]
        query_list = causal_query[shuffled]
        key_listed = causal_key[shuffled]
        rank = jnp.argsort(jnp.where(keep, 0, 1) * pair_total + jnp.arange(pair_total))
        query_list = query_list[rank]
        key_listed = key_listed[rank]
        keep = keep[rank]
        rotation = jax.random.randint(key_list[2], (), 0, SPAN)
        serial = jnp.arange(pair_total)
        device = (serial + rotation) % SPAN
        slot_number = serial // SPAN
        flat_index = jnp.where(keep, device * PCAP + slot_number, SPAN * PCAP)
        table_out = jnp.full((SPAN * PCAP, 2), -1, jnp.int32)
        return table_out.at[flat_index].set(jnp.stack([query_list, key_listed], axis=1).astype(jnp.int32), mode='drop')
    return jax.vmap(one_group)(jax.random.split(key, GROUPS)).astype(jnp.int32)


def levels(stream_key, extent, cuts, least, top_value):
    gain = 1.0
    for dim, shards_of in cuts:
        draws = jax.random.uniform(jax.random.fold_in(jax.random.fold_in(stream_key, 6), dim), (shards_of,), jnp.float32, least / len(cuts), top_value / len(cuts))
        gain = gain * jnp.repeat(jnp.exp(draws), extent[dim] // shards_of).reshape((-1,) + (1,) * (len(extent) - 1 - dim))
    return gain


def profile(number_of, total, limit, skew):
    portions = [(1 << 20) // math.isqrt(grade ** skew) + 1 for grade in range(2, number_of + 1)]
    spare, given = total - limit - (number_of - 1), [1] * (number_of - 1)
    while spare > 0:
        movable = [i for i in range(number_of - 1) if given[i] < limit]
        whole, remaining = sum([portions[i] for i in movable]), spare
        for i in movable:
            more = min(limit - given[i], max(1, remaining * portions[i] // whole), spare)
            given[i] = given[i] + more
            spare = spare - more
    return np.array([limit] + given)


def uneven_parts(rng, amount, total, bound, lean):
    if amount == 2:
        one = jax.random.randint(rng, (), max(1, total - bound), min(bound, total - 1) + 1)
        return jnp.stack([one, total - one])
    sizes = jnp.asarray(profile(amount, total, bound, lean), jnp.int32)
    couples = (amount - 1) // 2
    giver, taker = sizes[1:1 + 2 * couples:2], sizes[2:2 + 2 * couples:2]
    slack = jnp.minimum(giver - 1, bound - taker)
    shifted = jax.random.randint(jax.random.fold_in(rng, 1), (couples,), 0, 1 << 20) % (slack + 1)
    sizes = sizes.at[1:1 + 2 * couples:2].set(giver - shifted).at[2:2 + 2 * couples:2].set(taker + shifted)
    return sizes[jax.random.permutation(jax.random.fold_in(rng, 2), amount)]


def bell_draw(rng, shape, deviation, bound, pieces=(), kind=jnp.bfloat16):
    values = deviation * jax.random.normal(rng, shape, jnp.float32)
    if pieces:
        values = values * levels(rng, shape, pieces, -0.22, 0.18)
    return jnp.clip(values, -bound, bound).astype(kind)


def setup_inputs(seed: int = 0) -> dict:
    keys = jax.random.split(jax.random.key(seed), 9)
    table = bell_draw(keys[0], (ROWS, D), 1.0, 6.0, ((0, 32),), jnp.float32)
    accum = jnp.clip(jnp.exp(math.log(2.0) - 3.6888794 * jax.random.uniform(keys[1], (ROWS,), jnp.float32) ** levels(keys[1], (ROWS,), ((0, 32),), -0.2, 0.2)), 0.05, 2.0)
    item_row = draw_item_row(jax.random.fold_in(keys[8], 71), 0)
    segments = jax.vmap(lambda own: jnp.searchsorted(jnp.cumsum(uneven_parts(own, 2, GROUP_ROWS, GROUP_ROWS - TOK_DEV // 2, 2)), jnp.arange(GROUP_ROWS), side="right"))(jax.random.split(keys[3], GROUPS)).reshape((GROUPS, GROUP_ROWS)).astype(jnp.int32)
    pairs = draw_pairs(jax.random.fold_in(keys[8], 71), 0)
    w_in = bell_draw(keys[5], (D, 4 * D), D ** -0.5, 0.25)
    w_out = bell_draw(keys[6], (D, D), D ** -0.5, 0.25)
    out_grad = bell_draw(keys[7], (TOKENS, D), 1.0, 6.0, ((0, 32),))
    return dict(table=table, accum=accum, item_row=item_row, segments=segments, pairs=pairs, w_in=w_in, w_out=w_out, out_grad=out_grad)


norm_eps = 1e-05
learn_rate = 0.5

def normalize(values):
    row_mean = lax.optimization_barrier(jnp.mean(values, axis=-1, keepdims=True))
    centred = values - row_mean
    spread = jnp.sqrt(lax.optimization_barrier(jnp.mean(centred * centred, axis=-1, keepdims=True)) + norm_eps)
    return (centred / spread, spread)

def norm_back(grad_rows, normed, spread):
    first_mean = lax.optimization_barrier(jnp.mean(grad_rows, axis=-1, keepdims=True))
    second_mean = lax.optimization_barrier(jnp.mean(grad_rows * normed, axis=-1, keepdims=True))
    return (grad_rows - first_mean - normed * second_mean) / spread

def silu_slope(values):
    sigmoid_value = jax.nn.sigmoid(values)
    return sigmoid_value * (1.0 + values * (1.0 - sigmoid_value))

def round_trip(values):
    return lax.optimization_barrier(values.astype(jnp.bfloat16)).astype(jnp.float32)

def split_heads(matrix):
    return matrix.astype(jnp.float32).reshape(matrix.shape[0], HEADS, DH)

def block_visible(present_group, segment_group, block_index):
    query_pos = jnp.arange(TOK_DEV, dtype=jnp.int32) + block_index * TOK_DEV
    key_pos = jnp.arange(GROUP_ROWS, dtype=jnp.int32)
    listed = present_group[block_index][key_pos // TOK_DEV]
    same = segment_group[key_pos][None, :] == segment_group[query_pos][:, None]
    return listed[None, :] & (key_pos[None, :] <= query_pos[:, None]) & same

def group_forward(operands):
    hidden, segment_group, present_group = operands
    key_rows = split_heads(hidden[:, 3 * D:])
    value_rows = split_heads(hidden[:, D:2 * D])
    results = []
    for block_index in range(SPAN):
        visible = block_visible(present_group, segment_group, block_index)
        query_rows = split_heads(hidden[block_index * TOK_DEV:(block_index + 1) * TOK_DEV, 2 * D:3 * D])
        scores = jnp.einsum('rhd,chd->hrc', query_rows, key_rows) * DH ** (-0.5)
        weights = round_trip(jnp.where(visible[None], jax.nn.silu(scores), 0.0))
        results.append(jnp.einsum('hrc,chd->rhd', weights, value_rows).reshape(TOK_DEV, D))
    return jnp.concatenate(results, axis=0)

def group_backward(operands):
    hidden, grad_attend, segment_group, present_group = operands
    key_rows = split_heads(hidden[:, 3 * D:])
    value_rows = split_heads(hidden[:, D:2 * D])
    grad_key = jnp.zeros((GROUP_ROWS, HEADS, DH), jnp.float32)
    grad_value = jnp.zeros((GROUP_ROWS, HEADS, DH), jnp.float32)
    query_grads = []
    for block_index in range(SPAN):
        visible = block_visible(present_group, segment_group, block_index)
        lower = block_index * TOK_DEV
        upper = lower + TOK_DEV
        query_rows = split_heads(hidden[lower:upper, 2 * D:3 * D])
        grad_rows = split_heads(grad_attend[lower:upper])
        scores = jnp.einsum('rhd,chd->hrc', query_rows, key_rows) * DH ** (-0.5)
        weights = round_trip(jnp.where(visible[None], jax.nn.silu(scores), 0.0))
        grad_weights = jnp.einsum('rhd,chd->hrc', grad_rows, value_rows)
        grad_scores = round_trip(jnp.where(visible[None], grad_weights * silu_slope(scores) * DH ** (-0.5), 0.0))
        query_grads.append(jnp.einsum('hrc,chd->rhd', grad_scores, key_rows).reshape(TOK_DEV, D))
        grad_key = grad_key + jnp.einsum('hrc,rhd->chd', grad_scores, query_rows)
        grad_value = grad_value + jnp.einsum('hrc,rhd->chd', weights, grad_rows)
    return (jnp.concatenate(query_grads, axis=0), grad_key.reshape(GROUP_ROWS, D), grad_value.reshape(GROUP_ROWS, D))

def reference(table, accum, item_row, segments, pairs, w_in, w_out, out_grad):
    action_rows = table[item_row].astype(jnp.bfloat16)
    action_float = action_rows.astype(jnp.float32)
    normed, action_spread = normalize(action_float)
    normed_low = normed.astype(jnp.bfloat16)
    pre_act = jnp.dot(normed_low, w_in, preferred_element_type=jnp.float32)
    hidden = jax.nn.silu(pre_act).astype(jnp.bfloat16)
    blocks = jnp.arange(SPAN, dtype=jnp.int32)
    present = jnp.any((pairs[:, :, 0, None, None] == blocks[None, None, :, None]) & (pairs[:, :, 1, None, None] == blocks[None, None, None, :]), axis=1)
    grouped = hidden.reshape(GROUPS, GROUP_ROWS, 4 * D)
    attended = lax.map(group_forward, (grouped, segments, present)).reshape(TOKENS, D)
    attend_norm, attend_spread = normalize(attended)
    unit_gate = hidden[:, :D].astype(jnp.float32)
    gated = (attend_norm * unit_gate).astype(jnp.bfloat16)
    layer_sum = jnp.dot(gated, w_out, preferred_element_type=jnp.float32) + action_float
    layer_out = layer_sum.astype(jnp.bfloat16)
    grad_scale = TOKENS ** (-0.5)
    grad_out = jnp.dot(gated.T, out_grad, preferred_element_type=jnp.float32) * grad_scale
    grad_gated = jnp.dot(out_grad, w_out.T, preferred_element_type=jnp.float32)
    grad_attend = norm_back(grad_gated * unit_gate, attend_norm, attend_spread).astype(jnp.bfloat16)
    grad_query, grad_key, grad_value = lax.map(group_backward, (grouped, grad_attend.reshape(GROUPS, GROUP_ROWS, D), segments, present))
    grad_hidden = jnp.concatenate([grad_gated * attend_norm, grad_value.reshape(TOKENS, D), grad_query.reshape(TOKENS, D), grad_key.reshape(TOKENS, D)], axis=1)
    grad_pre = (grad_hidden * silu_slope(pre_act)).astype(jnp.bfloat16)
    grad_in = jnp.dot(normed_low.T, grad_pre, preferred_element_type=jnp.float32) * grad_scale
    grad_normed = jnp.dot(grad_pre, w_in.T, preferred_element_type=jnp.float32)
    grad_action = norm_back(grad_normed, normed, action_spread) + out_grad.astype(jnp.float32)
    row_total = jnp.zeros((ROWS, D), jnp.float32).at[item_row].add(grad_action)
    accum_new = accum + lax.optimization_barrier(jnp.mean(row_total * row_total, axis=1))
    table_new = table - learn_rate * row_total / jnp.sqrt(accum_new)[:, None]
    return (layer_out, table_new, accum_new, grad_in, grad_out)
```

```python
import functools
import math

import jax
import jax.numpy as jnp
from jax import lax
from jax.experimental import pallas as pl
from jax.experimental.pallas import tpu as pltpu
from jax.sharding import PartitionSpec as P

HEADS = 8
LANES = 128
CHUNK = 128
FAR = float(2**30)
VMEM_BYTES = 48 * 1024 * 1024

norm_eps = 1e-05
learn_rate = 0.5
f32 = jnp.float32
bf16 = jnp.bfloat16


def dot(left, right):
    return lax.dot_general(left, right, (((1,), (0,)), ((), ())), preferred_element_type=f32)


def dot_nt(left, right):
    return lax.dot_general(left, right, (((1,), (1,)), ((), ())), preferred_element_type=f32)


def normalize(values):
    row_mean = jnp.mean(values, axis=-1, keepdims=True)
    centred = values - row_mean
    spread = jnp.sqrt(jnp.mean(centred * centred, axis=-1, keepdims=True) + norm_eps)
    return (centred / spread, spread)


def norm_back(grad_rows, normed, spread):
    first_mean = jnp.mean(grad_rows, axis=-1, keepdims=True)
    second_mean = jnp.mean(grad_rows * normed, axis=-1, keepdims=True)
    return (grad_rows - first_mean - normed * second_mean) / spread


def silu(values):
    half = 0.5 * values
    return half + half * jnp.tanh(half)


def silu_slope(values):
    half = 0.5 * values
    curve = jnp.tanh(half)
    return (0.5 + 0.5 * curve) * (1.0 + half * (1.0 - curve))


def head_halves(width, rows):
    lane = lax.broadcasted_iota(jnp.int32, (rows, LANES), 1)
    return [(lane >= start) & (lane < start + width) for start in range(0, LANES, width)]


def join_heads(parts, halves):
    joined = parts[-1]
    for part, half in zip(parts[:-1], halves[:-1]):
        joined = jnp.where(half, part, joined)
    return joined


def at(ref, rows, group):
    return ref[rows, pl.ds(group * LANES, LANES)]


def causal(scores, first_row, lower):
    row = lax.broadcasted_iota(jnp.int32, scores.shape, 0) + first_row
    column = lax.broadcasted_iota(jnp.int32, scores.shape, 1)
    if lower:
        return jnp.where(column <= row, scores, -FAR)
    return jnp.where(row <= column + first_row, scores, -FAR)


def forward_pair(query, query_mask, key, value, key_mask, total, width, diagonal):
    tokens, model_width = query.shape
    scale = 0.5 / math.sqrt(width)
    halves = head_halves(width, CHUNK)
    for group in range(model_width // LANES):
        for first in range(0, tokens, CHUNK):
            rows = pl.ds(first, CHUNK)
            seen = pl.ds(0, first + CHUNK if diagonal else tokens)
            keys = jnp.concatenate([at(key, seen, group), key_mask[seen, :]], axis=1)
            values = at(value, seen, group)
            own = at(query, rows, group) * jnp.asarray(scale, bf16)
            parts = []
            for half in halves:
                queries = jnp.concatenate(
                    [jnp.where(half, own, jnp.zeros_like(own)), query_mask[rows, :]], axis=1
                )
                half_score = dot_nt(queries, keys)
                if diagonal:
                    half_score = causal(half_score, first, True)
                weights = half_score + half_score * jnp.tanh(half_score)
                parts.append(dot(weights.astype(bf16), values))
            total[rows, pl.ds(group * LANES, LANES)] += join_heads(parts, halves)


def query_pair(query, query_mask, grad, key, value, key_mask, total, width, diagonal):
    tokens, model_width = query.shape
    scale = 0.5 / math.sqrt(width)
    halves = head_halves(width, CHUNK)
    for group in range(model_width // LANES):
        for first in range(0, tokens, CHUNK):
            rows = pl.ds(first, CHUNK)
            seen = pl.ds(0, first + CHUNK if diagonal else tokens)
            keys = jnp.concatenate([at(key, seen, group), key_mask[seen, :]], axis=1)
            values = at(value, seen, group)
            own = at(query, rows, group) * jnp.asarray(scale, bf16)
            own_grad = at(grad, rows, group) * jnp.asarray(scale, bf16)
            parts = []
            for half in halves:
                queries = jnp.concatenate(
                    [jnp.where(half, own, jnp.zeros_like(own)), query_mask[rows, :]], axis=1
                )
                half_score = dot_nt(queries, keys)
                if diagonal:
                    half_score = causal(half_score, first, True)
                grad_weights = dot_nt(jnp.where(half, own_grad, jnp.zeros_like(own)), values)
                curve = jnp.tanh(half_score)
                slope = (1.0 + curve) * (1.0 + half_score * (1.0 - curve))
                grad_scores = (grad_weights * slope).astype(bf16)
                parts.append(dot(grad_scores, at(key, seen, group)))
            total[rows, pl.ds(group * LANES, LANES)] += join_heads(parts, halves)


def key_pair(
    query, query_mask, grad, key, value, key_mask, key_total, value_total, width, diagonal
):
    tokens, model_width = key.shape
    scale = 0.5 / math.sqrt(width)
    halves = head_halves(width, CHUNK)
    for group in range(model_width // LANES):
        for first in range(0, tokens, CHUNK):
            rows = pl.ds(first, CHUNK)
            start = first if diagonal else 0
            seen = pl.ds(start, tokens - start)
            queries = jnp.concatenate([at(query, seen, group), query_mask[seen, :]], axis=1)
            grads = at(grad, seen, group)
            own_key = at(key, rows, group) * jnp.asarray(scale, bf16)
            own_value = at(value, rows, group) * jnp.asarray(scale, bf16)
            key_parts, value_parts = [], []
            for half in halves:
                keys = jnp.concatenate(
                    [jnp.where(half, own_key, jnp.zeros_like(own_key)), key_mask[rows, :]], axis=1
                )
                half_score = dot_nt(keys, queries)
                if diagonal:
                    half_score = causal(half_score, first, False)
                grad_weights = dot_nt(jnp.where(half, own_value, jnp.zeros_like(own_key)), grads)
                curve = jnp.tanh(half_score)
                weights = half_score + half_score * curve
                slope = (1.0 + curve) * (1.0 + half_score * (1.0 - curve))
                grad_scores = (grad_weights * slope).astype(bf16)
                value_parts.append(dot(weights.astype(bf16), grads))
                key_parts.append(dot(grad_scores, at(query, seen, group)))
            key_total[rows, pl.ds(group * LANES, LANES)] += join_heads(key_parts, halves)
            value_total[rows, pl.ds(group * LANES, LANES)] += join_heads(value_parts, halves)


def near_kernel(
    width, place, seen, own, near, w_in, query_mask, key_mask, u_out, v_out, q_out, k_out, total,
    near_key, near_value,
):
    model_width = own.shape[1]
    me = place[0]
    for block, out in ((3, k_out), (1, v_out), (2, q_out), (0, u_out)):
        columns = pl.ds(block * model_width, model_width)
        out[...] = silu(dot(own[...], w_in[:, columns])).astype(bf16)
    total[...] = jnp.zeros_like(total)
    forward_pair(
        q_out, query_mask.at[me], k_out, v_out, key_mask.at[me], total, width, True
    )
    other = jnp.bitwise_xor(me, 1)

    @pl.when((other < me) & (seen[me, other] > 0))
    def _():
        value_columns = pl.ds(model_width, model_width)
        key_columns = pl.ds(3 * model_width, model_width)
        near_key[...] = silu(dot(near[...], w_in[:, key_columns])).astype(bf16)
        near_value[...] = silu(dot(near[...], w_in[:, value_columns])).astype(bf16)
        forward_pair(
            q_out, query_mask.at[me], near_key, near_value, key_mask.at[other], total, width, False
        )


def far_kernel(width, count, place, seen, *refs):
    far = refs[:count]
    (w_in, query, u_rows, query_mask, key_mask, near_total, out_grad, w_out) = refs[
        count : count + 8
    ]
    (attend_norm_out, grad_attend_out, total, far_key, far_value) = refs[count + 8 :]
    model_width = query.shape[1]
    me = place[0]
    total[...] = near_total[...]
    for index in range(count):
        other = jnp.bitwise_xor(me, index + 2)

        @pl.when((other < me) & (seen[me, other] > 0))
        def _():
            value_columns = pl.ds(model_width, model_width)
            key_columns = pl.ds(3 * model_width, model_width)
            rows = far[index]
            far_key[...] = silu(dot(rows[...], w_in[:, key_columns])).astype(bf16)
            far_value[...] = silu(dot(rows[...], w_in[:, value_columns])).astype(bf16)
            forward_pair(
                query, query_mask.at[me], far_key, far_value, key_mask.at[other], total, width,
                False,
            )

    attend_norm, attend_spread = normalize(total[...])
    unit_gate = u_rows[...].astype(f32)
    grad_gated = dot_nt(out_grad[...], w_out[...])
    attend_norm_out[...] = attend_norm
    grad_attend_out[...] = norm_back(grad_gated * unit_gate, attend_norm, attend_spread).astype(
        bf16
    )


def middle_kernel(
    factor, attend_norm, u_rows, out_grad, w_out, w_in, own, action, order, layer_out, grad_pre_out,
    early_out,
):
    model_width = own.shape[1]
    gated = (attend_norm[...] * u_rows[...].astype(f32)).astype(bf16)
    layer_out[...] = (dot(gated, w_out[...]) + action[...].astype(f32)).astype(bf16)
    grad_gated = dot_nt(out_grad[...], w_out[...])
    pre_act = dot(own[...], w_in[:, pl.ds(0, model_width)])
    grad_pre = (grad_gated * attend_norm[...] * silu_slope(pre_act)).astype(bf16)
    grad_pre_out[...] = grad_pre
    gated_turned = dot_nt(order[...], gated).astype(bf16)
    own_turned = dot_nt(order[...], own[...]).astype(bf16)
    early_out[:, pl.ds(0, model_width)] = dot(gated_turned, out_grad[...]) * factor
    early_out[:, pl.ds(model_width, model_width)] = dot(own_turned, grad_pre) * factor


def inner_kernel(
    width, count, place, seen, query, key, value, grad, query_mask, key_mask, w_in, *refs
):
    rows = refs[:count]
    query_total, key_total, value_total, far_key, far_value = refs[count:]
    model_width = query.shape[1]
    me = place[0]
    query_total[...] = jnp.zeros_like(query_total)
    key_total[...] = jnp.zeros_like(key_total)
    value_total[...] = jnp.zeros_like(value_total)
    query_pair(
        query, query_mask.at[me], grad, key, value, key_mask.at[me], query_total, width, True
    )
    key_pair(
        query, query_mask.at[me], grad, key, value, key_mask.at[me], key_total, value_total, width,
        True,
    )
    for index in range(count):
        other = jnp.bitwise_xor(me, index + 1)

        @pl.when((other < me) & (seen[me, other] > 0))
        def _():
            value_columns = pl.ds(model_width, model_width)
            key_columns = pl.ds(3 * model_width, model_width)
            far_key[...] = silu(dot(rows[index][...], w_in[:, key_columns])).astype(bf16)
            far_value[...] = silu(dot(rows[index][...], w_in[:, value_columns])).astype(bf16)
            query_pair(
                query, query_mask.at[me], grad, far_key, far_value, key_mask.at[other],
                query_total, width, False,
            )


def outer_kernel(
    width, count, place, seen, key, value, query_mask, key_mask, w_in, query_grad, key_grad,
    value_grad, own, action, out_grad, gate_grad_pre, *refs
):
    rows = refs[:count]
    grads = refs[count : 2 * count]
    (grad_pre_out, grad_action_out, key_total, value_total, far_query) = refs[2 * count :]
    model_width = key.shape[1]
    me = place[0]
    key_total[...] = key_grad[...]
    value_total[...] = value_grad[...]
    for index in range(count):
        other = jnp.bitwise_xor(me, index + 1)

        @pl.when((other > me) & (seen[other, me] > 0))
        def _():
            query_columns = pl.ds(2 * model_width, model_width)
            far_query[...] = silu(dot(rows[index][...], w_in[:, query_columns])).astype(bf16)
            key_pair(
                far_query, query_mask.at[other], grads[index], key, value, key_mask.at[me],
                key_total, value_total, width, False,
            )

    grad_normed = dot_nt(gate_grad_pre[...], w_in[:, pl.ds(0, model_width)])
    for block, source in ((1, value_total), (2, query_grad), (3, key_total)):
        columns = pl.ds(block * model_width, model_width)
        pre_act = dot(own[...], w_in[:, columns])
        grad_pre = (source[...] * silu_slope(pre_act)).astype(bf16)
        grad_pre_out[:, pl.ds((block - 1) * model_width, model_width)] = grad_pre
        grad_normed += dot_nt(grad_pre, w_in[:, columns])
    normed, spread = normalize(action[...].astype(f32))
    grad_action = norm_back(grad_normed, normed, spread) + out_grad[...].astype(f32)
    grad_action_out[...] = grad_action.astype(bf16)


def late_kernel(factor, own, order, grad_pre, late_out):
    own_turned = dot_nt(order[...], own[...]).astype(bf16)
    late_out[...] = dot(own_turned, grad_pre[...]) * factor


def call(kernel, name, scalars, arrays, outs, scratch=(), flops=0):
    touched = sum(math.prod(a.shape) * a.dtype.itemsize for a in list(arrays) + list(outs))
    return pl.pallas_call(
        kernel,
        name=name,
        out_shape=tuple(outs),
        in_specs=[pl.BlockSpec(memory_space=pltpu.SMEM)] * len(scalars)
        + [pl.BlockSpec(memory_space=pltpu.VMEM)] * len(arrays),
        out_specs=tuple([pl.BlockSpec(memory_space=pltpu.VMEM)] * len(outs)),
        scratch_shapes=list(scratch),
        compiler_params=pltpu.CompilerParams(vmem_limit_bytes=VMEM_BYTES),
        cost_estimate=pl.CostEstimate(flops=flops, bytes_accessed=touched, transcendentals=0),
    )(*scalars, *arrays)


def shaped(shape, dtype):
    return jax.ShapeDtypeStruct(shape, dtype)


def bits_of(size):
    return (size - 1).bit_length()


def swap(values, axis, bit, useful=None):
    count = lax.axis_size(axis)
    pairs = [(i, i ^ (1 << bit)) for i in range(count)]
    if useful is not None:
        pairs = [pair for pair in pairs if useful(*pair)]
    return lax.ppermute(values, axis, pairs)


def spread_blocks(own, axis, upward_only):
    count = lax.axis_size(axis)
    held = {0: own}
    for bit in reversed(range(bits_of(count))):
        for offset in sorted(held):
            keep = (lambda src, dst, offset=offset: (src ^ offset) > dst) if upward_only else None
            held[offset ^ (1 << bit)] = swap(held[offset], axis, bit, keep)
    return [held[offset] for offset in range(1, count)]


def halving_order():
    pair_bits, dp_bits = bits_of(lax.axis_size("pair")), bits_of(lax.axis_size("dp"))
    return [("pair", bit) for bit in range(pair_bits)] + [("dp", bit) for bit in range(dp_bits)]


def order_matrix(steps, model_width, shards):
    pair_bits = bits_of(lax.axis_size("pair"))
    each = model_width // shards
    place = jnp.arange(model_width, dtype=jnp.int32)
    block, within = place // each, place % each
    device = jnp.zeros_like(block)
    for depth, (axis, bit) in enumerate(steps):
        digit = (block >> (len(steps) - 1 - depth)) & 1
        device = device | (digit << (bit + (pair_bits if axis == "dp" else 0)))
    source = device * each + within
    return (source[:, None] == place[None, :]).astype(bf16)


def reduce_halving(values, steps):
    for axis, bit in steps:
        half = values.shape[0] // 2
        mine = (lax.axis_index(axis) >> bit) & 1
        sent = lax.dynamic_slice_in_dim(values, (1 - mine) * half, half, 0)
        kept = lax.dynamic_slice_in_dim(values, mine * half, half, 0)
        values = kept + swap(sent, axis, bit)
    return values


def body(table, accum, item_row, segments, pairs, w_in, w_out, out_grad):
    tokens = item_row.shape[0]
    rows_dev, model_width = table.shape
    shards = lax.axis_size(("dp", "pair"))
    span = lax.axis_size("pair")
    here = lax.axis_index("pair")
    bound_rows = 2 * (tokens // shards)
    width = model_width // HEADS
    factor = 1.0 / math.sqrt(tokens * shards)

    owner_ids = item_row // rows_dev
    row_slot = item_row % rows_dev
    shard_ids = jnp.arange(shards, dtype=jnp.int32)
    onehot = (owner_ids[:, None] == shard_ids[None, :]).astype(jnp.int32)
    bucket_rank = jnp.sum(jnp.cumsum(onehot, axis=0) * onehot, axis=1) - 1
    target = owner_ids * bound_rows + bucket_rank
    slots = jnp.arange(shards * bound_rows, dtype=jnp.int32)
    hits = slots[:, None] == target[None, :]
    request = jnp.sum(jnp.where(hits, row_slot[None, :], 0), axis=1).reshape(shards, bound_rows)
    slot_ids = lax.all_to_all(
        request, ("dp", "pair"), split_axis=0, concat_axis=0, tiled=True
    ).reshape(-1)
    table_places = jnp.arange(rows_dev, dtype=jnp.int32)
    found_rows = dot(
        (slot_ids[:, None] == table_places[None, :]).astype(bf16), table.astype(bf16)
    ).astype(bf16)
    fetched = lax.all_to_all(
        found_rows.reshape(shards, bound_rows, model_width),
        ("dp", "pair"), split_axis=0, concat_axis=0, tiled=True,
    ).reshape(shards * bound_rows, model_width)
    action = dot((target[:, None] == slots[None, :]).astype(bf16), fetched).astype(bf16)
    normed, _ = normalize(action.astype(f32))
    own = normed.astype(bf16)

    blocks = jnp.arange(span, dtype=jnp.int32)
    pair_list = pairs[0]
    present = jnp.any(
        (pair_list[:, 0, None, None] == blocks[None, :, None])
        & (pair_list[:, 1, None, None] == blocks[None, None, :]),
        axis=0,
    )
    block_segments = segments[0].reshape(span, tokens)
    reaches = block_segments[:, -1][None, :] >= block_segments[:, 0][:, None]
    seen = (present & reaches).astype(jnp.int32)
    place = here.astype(jnp.int32).reshape(1)
    lane = jnp.arange(LANES, dtype=jnp.int32)[None, None, :]
    later = (block_segments == 1)[:, :, None]
    first_lane, second_lane = lane == 0, lane == 1
    key_mask = jnp.where(
        (first_lane & ~later) | (second_lane & later), FAR, 0.0
    ).astype(bf16)
    query_mask = jnp.where(
        (first_lane & later) | (second_lane & ~later), -1.0, 0.0
    ).astype(bf16)
    scalars = (place, seen)

    wide_f32 = shaped((tokens, model_width), f32)
    wide_bf16 = shaped((tokens, model_width), bf16)
    scratch_f32 = pltpu.VMEM((tokens, model_width), f32)
    scratch_bf16 = pltpu.VMEM((tokens, model_width), bf16)
    pair_flops = 2 * tokens * tokens * model_width * 4

    rows = spread_blocks(own, "pair", False)
    count = span - 1
    u_rows, value, query, key, near_total = call(
        functools.partial(near_kernel, width), "near_attention", scalars,
        (own, rows[0], w_in, query_mask, key_mask),
        (wide_bf16, wide_bf16, wide_bf16, wide_bf16, wide_f32),
        (scratch_bf16, scratch_bf16),
        flops=4 * pair_flops,
    )
    attend_norm, grad_attend = call(
        functools.partial(far_kernel, width, count - 1), "far_attention", scalars,
        (*rows[1:], w_in, query, u_rows, query_mask, key_mask, near_total, out_grad, w_out),
        (wide_f32, wide_bf16),
        (scratch_f32, scratch_bf16, scratch_bf16),
        flops=4 * pair_flops,
    )
    grads = spread_blocks(grad_attend, "pair", True)
    steps = halving_order()
    order = order_matrix(steps, model_width, shards)
    layer_out, gate_grad_pre, early = call(
        functools.partial(middle_kernel, factor), "gate_gradients", (),
        (attend_norm, u_rows, out_grad, w_out, w_in, own, action, order),
        (wide_bf16, wide_bf16, shaped((model_width, 2 * model_width), f32)),
        flops=4 * pair_flops,
    )
    query_grad, key_grad, value_grad = call(
        functools.partial(inner_kernel, width, count), "query_gradients", scalars,
        (query, key, value, grad_attend, query_mask, key_mask, w_in, *rows),
        (wide_f32, wide_f32, wide_f32),
        (scratch_bf16, scratch_bf16),
        flops=12 * pair_flops,
    )
    early_sum = reduce_halving(early, steps)
    grad_pre, grad_action = call(
        functools.partial(outer_kernel, width, count), "key_gradients", scalars,
        (
            key, value, query_mask, key_mask, w_in, query_grad, key_grad, value_grad, own, action,
            out_grad, gate_grad_pre, *rows, *grads,
        ),
        (shaped((tokens, 3 * model_width), bf16), wide_bf16),
        (scratch_f32, scratch_f32, scratch_bf16),
        flops=12 * pair_flops,
    )
    sending = dot(hits.astype(bf16), grad_action).astype(bf16)
    returned = lax.all_to_all(
        sending.reshape(shards, bound_rows, model_width),
        ("dp", "pair"), split_axis=0, concat_axis=0, tiled=True,
    ).reshape(shards * bound_rows, model_width)
    (late,) = call(
        functools.partial(late_kernel, factor), "late_gradients", (),
        (own, order, grad_pre),
        (shaped((model_width, 3 * model_width), f32),),
        flops=2 * tokens * model_width * 4 * model_width,
    )
    late_sum = reduce_halving(late, steps)
    row_total = dot((table_places[:, None] == slot_ids[None, :]).astype(bf16), returned)
    accum_new = accum + jnp.mean(row_total * row_total, axis=1)
    table_new = table - learn_rate * row_total / jnp.sqrt(accum_new)[:, None]
    grad_in = jnp.concatenate([early_sum[:, model_width:], late_sum], axis=1)
    return (layer_out, table_new, accum_new, grad_in, early_sum[:, :model_width])


def solution(mesh):
    placed = (
        P(("dp", "pair"), None),
        P(("dp", "pair")),
        P(("dp", "pair")),
        P("dp", None),
        P("dp", None, None),
        P(),
        P(),
        P(("dp", "pair"), None),
    )
    return jax.shard_map(
        body,
        mesh=mesh,
        in_specs=placed,
        out_specs=(
            P(("dp", "pair"), None),
            P(("dp", "pair"), None),
            P(("dp", "pair")),
            P(("dp", "pair"), None),
            P(("dp", "pair"), None),
        ),
        check_vma=False,
    )
```

```python
import functools
import math

import jax
import jax.numpy as jnp
from jax import lax
from jax.experimental import pallas as pl
from jax.experimental.pallas import tpu as pltpu
from jax.sharding import PartitionSpec as P

HEADS = 8
LANES = 128
UNROLL = 4
FAR = float(2**30)
NARROW = (("dp", 0), ("pair", 1))
VMEM_BYTES = 20 * 1024 * 1024

norm_eps = 1e-05
learn_rate = 0.5
f32 = jnp.float32
bf16 = jnp.bfloat16


def dot(left, right):
    return lax.dot_general(left, right, (((1,), (0,)), ((), ())), preferred_element_type=f32)


def dot_nt(left, right):
    return lax.dot_general(left, right, (((1,), (1,)), ((), ())), preferred_element_type=f32)


def normalize(values):
    row_mean = jnp.mean(values, axis=-1, keepdims=True)
    centred = values - row_mean
    spread = jnp.sqrt(jnp.mean(centred * centred, axis=-1, keepdims=True) + norm_eps)
    return (centred / spread, spread)


def norm_back(grad_rows, normed, spread):
    first_mean = jnp.mean(grad_rows, axis=-1, keepdims=True)
    second_mean = jnp.mean(grad_rows * normed, axis=-1, keepdims=True)
    return (grad_rows - first_mean - normed * second_mean) / spread


def silu(values):
    half = 0.5 * values
    return half + half * jnp.tanh(half)


def silu_slope(values):
    half = 0.5 * values
    curve = jnp.tanh(half)
    return (0.5 + 0.5 * curve) * (1.0 + half * (1.0 - curve))


def head_halves(width, rows):
    lane = lax.broadcasted_iota(jnp.int32, (rows, LANES), 1)
    return [(lane >= start) & (lane < start + width) for start in range(0, LANES, width)]


def causal(scores, tokens, lower):
    row = lax.broadcasted_iota(jnp.int32, scores.shape, 0)
    column = lax.broadcasted_iota(jnp.int32, scores.shape, 1) % tokens
    return jnp.where(column <= row if lower else row <= column, scores, -FAR)


def apart(rows, halves):
    nothing = jnp.zeros_like(rows)
    return jnp.concatenate([jnp.where(half, rows, nothing) for half in halves], axis=0)


def widened(rows, mask):
    return jnp.concatenate([rows, mask], axis=1)


def scaled(rows, width):
    return rows * jnp.asarray(0.5 / math.sqrt(width), bf16)


def each_group(model_width, step):
    def one(group, carry):
        step(pl.ds(pl.multiple_of(group * LANES, LANES), LANES))
        return carry

    lax.fori_loop(0, model_width // LANES, one, 0, unroll=UNROLL)


def forward_pair(query, query_mask, key, value, key_mask, total, width, diagonal):
    tokens, model_width = query.shape
    halves = head_halves(width, tokens)
    mask_keys = jnp.concatenate([key_mask[...]] * len(halves), axis=0)

    def step(lanes):
        keys = widened(apart(scaled(key[:, lanes], width), halves), mask_keys)
        half_score = dot_nt(widened(query[:, lanes], query_mask[...]), keys)
        if diagonal:
            half_score = causal(half_score, tokens, True)
        weights = half_score + half_score * jnp.tanh(half_score)
        total[:, lanes] += dot(weights.astype(bf16), apart(value[:, lanes], halves))

    each_group(model_width, step)


def query_pair(query, query_mask, grad, key, value, key_mask, total, width, diagonal):
    tokens, model_width = query.shape
    halves = head_halves(width, tokens)
    mask_keys = jnp.concatenate([key_mask[...]] * len(halves), axis=0)

    def step(lanes):
        plain_keys = apart(key[:, lanes], halves)
        keys = widened(scaled(plain_keys, width), mask_keys)
        half_score = dot_nt(widened(query[:, lanes], query_mask[...]), keys)
        if diagonal:
            half_score = causal(half_score, tokens, True)
        grad_weights = dot_nt(grad[:, lanes], apart(scaled(value[:, lanes], width), halves))
        curve = 1.0 + jnp.tanh(half_score)
        slope = curve * (1.0 + half_score * (2.0 - curve))
        total[:, lanes] += dot((grad_weights * slope).astype(bf16), plain_keys)

    each_group(model_width, step)


def key_pair(
    query, query_mask, grad, key, value, key_mask, key_total, value_total, width, diagonal
):
    tokens, model_width = key.shape
    halves = head_halves(width, tokens)
    mask_queries = jnp.concatenate([query_mask[...]] * len(halves), axis=0)

    def step(lanes):
        plain_queries = apart(query[:, lanes], halves)
        queries = widened(plain_queries, mask_queries)
        grads = apart(grad[:, lanes], halves)
        half_score = dot_nt(widened(scaled(key[:, lanes], width), key_mask[...]), queries)
        if diagonal:
            half_score = causal(half_score, tokens, False)
        grad_weights = dot_nt(scaled(value[:, lanes], width), grads)
        curve = 1.0 + jnp.tanh(half_score)
        weights = half_score * curve
        slope = curve + weights * (2.0 - curve)
        value_total[:, lanes] += dot(weights.astype(bf16), grads)
        key_total[:, lanes] += dot((grad_weights * slope).astype(bf16), plain_queries)

    each_group(model_width, step)


def near_kernel(
    width, place, seen, own, near, w_in, query_mask, key_mask, u_out, v_out, q_out, k_out, total,
    near_key, near_value,
):
    model_width = own.shape[1]
    me = place[0]
    for block, out in ((3, k_out), (1, v_out), (2, q_out), (0, u_out)):
        columns = pl.ds(block * model_width, model_width)
        out[...] = silu(dot(own[...], w_in[:, columns])).astype(bf16)
    total[...] = jnp.zeros_like(total)
    forward_pair(
        q_out, query_mask.at[me], k_out, v_out, key_mask.at[me], total, width, True
    )
    other = jnp.bitwise_xor(me, 1)

    @pl.when((other < me) & (seen[me, other] > 0))
    def _():
        value_columns = pl.ds(model_width, model_width)
        key_columns = pl.ds(3 * model_width, model_width)
        near_key[...] = silu(dot(near[...], w_in[:, key_columns])).astype(bf16)
        near_value[...] = silu(dot(near[...], w_in[:, value_columns])).astype(bf16)
        forward_pair(
            q_out, query_mask.at[me], near_key, near_value, key_mask.at[other], total, width, False
        )


def split_product(turned, right, half_bit, kept_out, sent_out, columns):
    half = turned.shape[0] // 2
    kept_rows = pl.ds(pl.multiple_of(half_bit * half, half), half)
    sent_rows = pl.ds(pl.multiple_of((1 - half_bit) * half, half), half)
    sent_out[:, columns] = dot(turned[sent_rows, :], right)
    kept_out[:, columns] = dot(turned[kept_rows, :], right)


def far_kernel(width, count, place, seen, *refs):
    far = refs[:count]
    (w_in, query, u_rows, query_mask, key_mask, near_total, out_grad, w_out, own, action, order) = (
        refs[count : count + 11]
    )
    (
        grad_attend_out, layer_out, gate_grad_pre, kept_out, sent_out, total, far_key, far_value,
        turned,
    ) = refs[count + 11 :]
    model_width = query.shape[1]
    me = place[0]
    total[...] = near_total[...]
    for index in range(count):
        other = jnp.bitwise_xor(me, index + 2)

        @pl.when((other < me) & (seen[me, other] > 0))
        def _():
            value_columns = pl.ds(model_width, model_width)
            key_columns = pl.ds(3 * model_width, model_width)
            rows = far[index]
            far_key[...] = silu(dot(rows[...], w_in[:, key_columns])).astype(bf16)
            far_value[...] = silu(dot(rows[...], w_in[:, value_columns])).astype(bf16)
            forward_pair(
                query, query_mask.at[me], far_key, far_value, key_mask.at[other], total, width,
                False,
            )

    attend_norm, attend_spread = normalize(total[...])
    unit_gate = u_rows[...].astype(f32)
    grad_gated = dot_nt(out_grad[...], w_out[...])
    grad_attend_out[...] = norm_back(grad_gated * unit_gate, attend_norm, attend_spread).astype(
        bf16
    )
    gated = (attend_norm * unit_gate).astype(bf16)
    layer_out[...] = (dot(gated, w_out[...]) + action[...].astype(f32)).astype(bf16)
    pre_act = dot(own[...], w_in[:, pl.ds(0, model_width)])
    grad_pre = (grad_gated * attend_norm * silu_slope(pre_act)).astype(bf16)
    gate_grad_pre[...] = grad_pre
    half_bit = jnp.bitwise_and(me, 1)
    turned[...] = dot_nt(order[...], gated).astype(bf16)
    split_product(turned, out_grad[...], half_bit, kept_out, sent_out, pl.ds(0, model_width))
    turned[...] = dot_nt(order[...], own[...]).astype(bf16)
    split_product(turned, grad_pre, half_bit, kept_out, sent_out, pl.ds(model_width, model_width))


def inner_kernel(
    width, count, place, seen, query, key, value, grad, query_mask, key_mask, w_in, own,
    gate_grad_pre, order, near_grad, *refs
):
    rows = refs[:count]
    (
        normed_total, key_total, value_total, kept_out, sent_out, query_total, far_key, far_value,
        turned,
    ) = refs[count:]
    model_width = query.shape[1]
    me = place[0]
    query_total[...] = jnp.zeros_like(query_total)
    key_total[...] = jnp.zeros_like(key_total)
    value_total[...] = jnp.zeros_like(value_total)
    query_pair(
        query, query_mask.at[me], grad, key, value, key_mask.at[me], query_total, width, True
    )
    key_pair(
        query, query_mask.at[me], grad, key, value, key_mask.at[me], key_total, value_total, width,
        True,
    )
    for index in range(count):
        other = jnp.bitwise_xor(me, index + 1)

        @pl.when((other < me) & (seen[me, other] > 0))
        def _():
            value_columns = pl.ds(model_width, model_width)
            key_columns = pl.ds(3 * model_width, model_width)
            far_key[...] = silu(dot(rows[index][...], w_in[:, key_columns])).astype(bf16)
            far_value[...] = silu(dot(rows[index][...], w_in[:, value_columns])).astype(bf16)
            query_pair(
                query, query_mask.at[me], grad, far_key, far_value, key_mask.at[other],
                query_total, width, False,
            )

    other = jnp.bitwise_xor(me, 1)

    @pl.when((other > me) & (seen[other, me] > 0))
    def _():
        far_key[...] = silu(dot(rows[0][...], w_in[:, pl.ds(2 * model_width, model_width)])).astype(
            bf16
        )
        key_pair(
            far_key, query_mask.at[other], near_grad, key, value, key_mask.at[me], key_total,
            value_total, width, False,
        )

    gate_columns = pl.ds(0, model_width)
    query_columns = pl.ds(2 * model_width, model_width)
    pre_act = dot(own[...], w_in[:, query_columns])
    grad_pre = (query_total[...] * silu_slope(pre_act)).astype(bf16)
    normed_total[...] = dot_nt(gate_grad_pre[...], w_in[:, gate_columns]) + dot_nt(
        grad_pre, w_in[:, query_columns]
    )
    turned[...] = dot_nt(order[...], own[...]).astype(bf16)
    split_product(
        turned, grad_pre, jnp.bitwise_and(me, 1), kept_out, sent_out, pl.ds(0, model_width)
    )


def outer_kernel(
    width, count, place, seen, key, value, query_mask, key_mask, w_in, normed_part, key_grad,
    value_grad, own, action, out_grad, order, target, *refs
):
    rows = refs[:count]
    grads = refs[count : 2 * count]
    (sending, kept_out, sent_out, key_total, value_total, far_query, turned) = refs[2 * count :]
    model_width = key.shape[1]
    me = place[0]
    key_total[...] = key_grad[...]
    value_total[...] = value_grad[...]
    for index in range(count):
        other = jnp.bitwise_xor(me, index + 2)

        @pl.when((other > me) & (seen[other, me] > 0))
        def _():
            query_columns = pl.ds(2 * model_width, model_width)
            far_query[...] = silu(dot(rows[index][...], w_in[:, query_columns])).astype(bf16)
            key_pair(
                far_query, query_mask.at[other], grads[index], key, value, key_mask.at[me],
                key_total, value_total, width, False,
            )

    half_bit = jnp.bitwise_and(me, 1)
    turned[...] = dot_nt(order[...], own[...]).astype(bf16)
    grad_normed = normed_part[...]
    for place_out, (block, source) in enumerate(((1, value_total), (3, key_total))):
        columns = pl.ds(block * model_width, model_width)
        pre_act = dot(own[...], w_in[:, columns])
        grad_pre = (source[...] * silu_slope(pre_act)).astype(bf16)
        grad_normed += dot_nt(grad_pre, w_in[:, columns])
        split_product(
            turned, grad_pre, half_bit, kept_out, sent_out,
            pl.ds(place_out * model_width, model_width),
        )
    normed, spread = normalize(action[...].astype(f32))
    grad_action = norm_back(grad_normed, normed, spread) + out_grad[...].astype(f32)
    slot = lax.broadcasted_iota(jnp.int32, (sending.shape[0], key.shape[0]), 0)
    hits = jnp.where(slot == target[...], 1.0, 0.0).astype(bf16)
    sending[...] = dot(hits, grad_action.astype(bf16)).astype(bf16)


def call(kernel, name, scalars, arrays, outs, scratch=(), flops=0, vmem=VMEM_BYTES):
    touched = sum(math.prod(a.shape) * a.dtype.itemsize for a in list(arrays) + list(outs))
    return pl.pallas_call(
        kernel,
        name=name,
        out_shape=tuple(outs),
        in_specs=[pl.BlockSpec(memory_space=pltpu.SMEM)] * len(scalars)
        + [pl.BlockSpec(memory_space=pltpu.VMEM)] * len(arrays),
        out_specs=tuple([pl.BlockSpec(memory_space=pltpu.VMEM)] * len(outs)),
        scratch_shapes=list(scratch),
        compiler_params=pltpu.CompilerParams(vmem_limit_bytes=vmem),
        cost_estimate=pl.CostEstimate(flops=flops, bytes_accessed=touched, transcendentals=0),
    )(*scalars, *arrays)


def shaped(shape, dtype):
    return jax.ShapeDtypeStruct(shape, dtype)


def bits_of(size):
    return (size - 1).bit_length()


def swap(values, axis, bit, useful=None):
    count = lax.axis_size(axis)
    pairs = [(i, i ^ (1 << bit)) for i in range(count)]
    if useful is not None:
        pairs = [pair for pair in pairs if useful(*pair)]
    return lax.ppermute(values, axis, pairs)


def spread_own(own, axis, upward_only):
    return spread_step({0: own}, [0], axis, upward_only)


def spread_step(held, offsets, axis, upward_only):
    held = dict(held)
    for bit in reversed(range(bits_of(lax.axis_size(axis)))):
        for offset in offsets:
            if offset & ((2 << bit) - 1) == 0 and offset ^ (1 << bit) not in held:
                keep = (lambda src, dst: (src ^ offset) > dst) if upward_only else None
                held[offset ^ (1 << bit)] = swap(held[offset], axis, bit, keep)
    return held


def spread_rest(held, axis, upward_only):
    while len(held) < lax.axis_size(axis):
        held = spread_step(held, sorted(set(held) - {0}), axis, upward_only)
    return [held[offset] for offset in range(1, lax.axis_size(axis))]


def after(values, witness):
    return lax.optimization_barrier((values, witness))[0]


def halving_steps():
    pair_bits, dp_bits = bits_of(lax.axis_size("pair")), bits_of(lax.axis_size("dp"))
    first = [("pair", 0), ("dp", 0)]
    pair_rest = [("pair", bit) for bit in range(1, pair_bits)]
    return first + pair_rest + [("dp", bit) for bit in range(1, dp_bits)]


def order_matrix(model_width, shards, steps):
    pair_bits = bits_of(lax.axis_size("pair"))
    each = model_width // shards
    place = jnp.arange(model_width, dtype=jnp.int32)
    device = jnp.zeros_like(place)
    for depth, (axis, bit) in enumerate(steps):
        digit = (place // each >> (len(steps) - 1 - depth)) & 1
        device = device | (digit << (bit + (pair_bits if axis == "dp" else 0)))
    source = device * each + place % each
    return (source[:, None] == place[None, :]).astype(bf16)


class Halving:
    def __init__(self, kept, sent, steps):
        self.steps = steps
        self.kept, self.received = kept, swap(sent, *steps[0])

    def half(self, which):
        axis, bit = self.steps[1]
        size = self.kept.shape[0] // 2
        mine = (lax.axis_index(axis) >> bit) & 1
        start = (mine if which == "kept" else 1 - mine) * size
        return lax.dynamic_slice_in_dim(self.kept, start, size, 0) + lax.dynamic_slice_in_dim(
            self.received, start, size, 0
        ).astype(f32)

    def leaving(self):
        sent = self.half("sent")
        return sent.astype(bf16) if self.steps[1] in NARROW else sent

    def step(self, sent=None):
        kept = self.half("kept")
        return Halving(kept, self.leaving() if sent is None else sent, self.steps[1:])

    def total(self):
        return self.kept + self.received.astype(f32)


def beside(left, right):
    joined = object.__new__(Halving)
    joined.steps = left.steps
    joined.kept = jnp.concatenate([left.kept, right.kept], axis=1)
    joined.received = jnp.concatenate([left.received, right.received], axis=1)
    return joined


def body(table, accum, item_row, segments, pairs, w_in, w_out, out_grad):
    tokens = item_row.shape[0]
    rows_dev, model_width = table.shape
    shards = lax.axis_size(("dp", "pair"))
    span = lax.axis_size("pair")
    here = lax.axis_index("pair")
    bound_rows = 2 * (tokens // shards)
    width = model_width // HEADS
    factor = 1.0 / math.sqrt(tokens * shards)

    owner_ids = item_row // rows_dev
    row_slot = item_row % rows_dev
    shard_ids = jnp.arange(shards, dtype=jnp.int32)
    onehot = (owner_ids[:, None] == shard_ids[None, :]).astype(jnp.int32)
    bucket_rank = jnp.sum(jnp.cumsum(onehot, axis=0) * onehot, axis=1) - 1
    target = owner_ids * bound_rows + bucket_rank
    slots = jnp.arange(shards * bound_rows, dtype=jnp.int32)
    hits = slots[:, None] == target[None, :]
    request = jnp.sum(jnp.where(hits, row_slot[None, :], 0), axis=1).reshape(shards, bound_rows)
    slot_ids = lax.all_to_all(
        request, ("dp", "pair"), split_axis=0, concat_axis=0, tiled=True
    ).reshape(-1)
    table_places = jnp.arange(rows_dev, dtype=jnp.int32)
    found_rows = dot(
        (slot_ids[:, None] == table_places[None, :]).astype(bf16), table.astype(bf16)
    ).astype(bf16)
    fetched = lax.all_to_all(
        found_rows.reshape(shards, bound_rows, model_width),
        ("dp", "pair"), split_axis=0, concat_axis=0, tiled=True,
    ).reshape(shards * bound_rows, model_width)
    action = dot((target[:, None] == slots[None, :]).astype(bf16), fetched).astype(bf16)
    normed, _ = normalize(action.astype(f32))
    own = normed.astype(bf16)

    blocks = jnp.arange(span, dtype=jnp.int32)
    pair_list = pairs[0]
    present = jnp.any(
        (pair_list[:, 0, None, None] == blocks[None, :, None])
        & (pair_list[:, 1, None, None] == blocks[None, None, :]),
        axis=0,
    )
    block_segments = segments[0].reshape(span, tokens)
    reaches = block_segments[:, -1][None, :] >= block_segments[:, 0][:, None]
    seen = (present & reaches).astype(jnp.int32)
    place = here.astype(jnp.int32).reshape(1)
    lane = jnp.arange(LANES, dtype=jnp.int32)[None, None, :]
    later = (block_segments == 1)[:, :, None]
    first_lane, second_lane = lane == 0, lane == 1
    key_mask = jnp.where(
        (first_lane & ~later) | (second_lane & later), FAR, 0.0
    ).astype(bf16)
    query_mask = jnp.where(
        (first_lane & later) | (second_lane & ~later), -1.0, 0.0
    ).astype(bf16)
    scalars = (place, seen)

    wide_f32 = shaped((tokens, model_width), f32)
    wide_bf16 = shaped((tokens, model_width), bf16)
    scratch_f32 = pltpu.VMEM((tokens, model_width), f32)
    scratch_bf16 = pltpu.VMEM((tokens, model_width), bf16)
    pair_flops = 2 * tokens * tokens * model_width * 4

    held = spread_own(own, "pair", False)
    count = span - 1
    u_rows, value, query, key, near_total = call(
        functools.partial(near_kernel, width), "near_attention", scalars,
        (own, held[1], w_in, query_mask, key_mask),
        (wide_bf16, wide_bf16, wide_bf16, wide_bf16, wide_f32),
        (scratch_bf16, scratch_bf16),
        flops=4 * pair_flops,
    )
    held = {0: own, 1: held[1], **after({k: v for k, v in held.items() if k > 1}, near_total)}
    rows = spread_rest(held, "pair", False)
    steps = halving_steps()
    order = order_matrix(model_width, shards, steps)
    half_width = model_width // 2
    scratch_turned = pltpu.VMEM((model_width, tokens), bf16)
    early_part = shaped((half_width, 2 * model_width), f32)
    middle_part = shaped((half_width, model_width), f32)
    late_part = shaped((half_width, 2 * model_width), f32)
    grad_attend, layer_out, gate_grad_pre, early_kept, early_sent = call(
        functools.partial(far_kernel, width, count - 1), "far_attention", scalars,
        (
            *rows[1:], w_in, query, u_rows, query_mask, key_mask, near_total, out_grad, w_out, own,
            action, order,
        ),
        (wide_bf16, wide_bf16, wide_bf16, early_part, early_part),
        (scratch_f32, scratch_bf16, scratch_bf16, scratch_turned),
        flops=4 * pair_flops,
    )
    held = spread_own(grad_attend, "pair", True)
    early = Halving(early_kept, early_sent, steps)
    normed_part, key_grad, value_grad, query_kept, query_sent = call(
        functools.partial(inner_kernel, width, count), "query_gradients", scalars,
        (
            query, key, value, grad_attend, query_mask, key_mask, w_in, own, gate_grad_pre,
            order, held[1], *rows,
        ),
        (wide_f32, wide_f32, wide_f32, middle_part, middle_part),
        (scratch_f32, scratch_bf16, scratch_bf16, scratch_turned),
        flops=12 * pair_flops,
    )
    held = {0: grad_attend, **after({k: v for k, v in held.items() if k > 0}, normed_part)}
    grads = spread_rest(held, "pair", True)
    middle = Halving(query_kept, query_sent, steps)
    early.received = after(early.received, normed_part)
    early_leaving, grads = lax.optimization_barrier((early.leaving(), grads))
    sending, late_kept, late_sent = call(
        functools.partial(outer_kernel, width, count - 1), "key_gradients", scalars,
        (
            key, value, query_mask, key_mask, w_in, normed_part, key_grad, value_grad, own, action,
            out_grad, order, target.reshape(1, tokens), *rows[1:], *grads[1:],
        ),
        (shaped((shards * bound_rows, model_width), bf16), late_part, late_part),
        (scratch_f32, scratch_f32, scratch_bf16, scratch_turned),
        flops=12 * pair_flops,
        vmem=3 * VMEM_BYTES,
    )
    early = early.step(early_leaving)
    late = Halving(late_kept, late_sent, steps)
    returned = lax.all_to_all(
        sending.reshape(shards, bound_rows, model_width),
        ("dp", "pair"), split_axis=0, concat_axis=0, tiled=True,
    ).reshape(shards * bound_rows, model_width)
    first = beside(early, middle.step())
    while len(first.steps) > 1:
        late = late.step()
        first = first.step()
    first, late = first.total(), late.step().total()
    grad_out = first[:, :model_width] * factor
    grad_in = factor * jnp.concatenate(
        [
            first[:, model_width : 2 * model_width], late[:, :model_width],
            first[:, 2 * model_width :], late[:, model_width:],
        ],
        axis=1,
    )
    row_total = dot((table_places[:, None] == slot_ids[None, :]).astype(bf16), returned)
    accum_new = accum + jnp.mean(row_total * row_total, axis=1)
    table_new = table - learn_rate * row_total / jnp.sqrt(accum_new)[:, None]
    return (layer_out, table_new, accum_new, grad_in, grad_out)


def solution(mesh):
    placed = (
        P(("dp", "pair"), None),
        P(("dp", "pair")),
        P(("dp", "pair")),
        P("dp", None),
        P("dp", None, None),
        P(),
        P(),
        P(("dp", "pair"), None),
    )
    return jax.shard_map(
        body,
        mesh=mesh,
        in_specs=placed,
        out_specs=(
            P(("dp", "pair"), None),
            P(("dp", "pair"), None),
            P(("dp", "pair")),
            P(("dp", "pair"), None),
            P(("dp", "pair"), None),
        ),
        check_vma=False,
    )
```

```python
import functools
import math

import jax
import jax.numpy as jnp
from jax import lax
from jax.experimental import pallas as pl
from jax.experimental.pallas import tpu as pltpu
from jax.sharding import PartitionSpec as P

HEADS = 8
LANES = 128
UNROLL = 4
FAR = float(2**30)
VMEM_BYTES = 20 * 1024 * 1024

norm_eps = 1e-05
learn_rate = 0.5
f32 = jnp.float32
bf16 = jnp.bfloat16


def dot(left, right):
    return lax.dot_general(left, right, (((1,), (0,)), ((), ())), preferred_element_type=f32)


def dot_nt(left, right):
    return lax.dot_general(left, right, (((1,), (1,)), ((), ())), preferred_element_type=f32)


def normalize(values):
    row_mean = jnp.mean(values, axis=-1, keepdims=True)
    centred = values - row_mean
    spread = jnp.sqrt(jnp.mean(centred * centred, axis=-1, keepdims=True) + norm_eps)
    return (centred / spread, spread)


def norm_back(grad_rows, normed, spread):
    first_mean = jnp.mean(grad_rows, axis=-1, keepdims=True)
    second_mean = jnp.mean(grad_rows * normed, axis=-1, keepdims=True)
    return (grad_rows - first_mean - normed * second_mean) / spread


def silu(values):
    half = 0.5 * values
    return half + half * jnp.tanh(half)


def silu_slope(values):
    half = 0.5 * values
    curve = jnp.tanh(half)
    return (0.5 + 0.5 * curve) * (1.0 + half * (1.0 - curve))


def head_halves(width, rows):
    lane = lax.broadcasted_iota(jnp.int32, (rows, LANES), 1)
    return [(lane >= start) & (lane < start + width) for start in range(0, LANES, width)]


def causal(scores, columns, lead, lower):
    row = lax.broadcasted_iota(jnp.int32, scores.shape, 0) + lead
    column = lax.broadcasted_iota(jnp.int32, scores.shape, 1) % columns
    return jnp.where(column <= row if lower else row <= column, scores, -FAR)


def apart(rows, halves):
    nothing = jnp.zeros_like(rows)
    return jnp.concatenate([jnp.where(half, rows, nothing) for half in halves], axis=0)


def widened(rows, mask):
    return jnp.concatenate([rows, mask], axis=1)


def scaled(rows, width):
    return rows * jnp.asarray(0.5 / math.sqrt(width), bf16)


def each_group(model_width, step):
    def one(group, carry):
        step(pl.ds(pl.multiple_of(group * LANES, LANES), LANES))
        return carry

    lax.fori_loop(0, model_width // LANES, one, 0, unroll=UNROLL)


def diagonal_spans(tokens, diagonal, lower):
    if not diagonal:
        return [(0, tokens, 0, tokens)]
    cut = tokens - LANES if lower else LANES
    if lower:
        return [(0, cut, 0, cut), (cut, tokens - cut, 0, tokens)]
    return [(0, cut, 0, tokens), (cut, tokens - cut, cut, tokens - cut)]


def forward_pair(query, query_mask, key, value, key_mask, total, width, diagonal):
    tokens, model_width = query.shape

    def step(lanes):
        for first, rows, start, columns in diagonal_spans(tokens, diagonal, True):
            own, seen = pl.ds(first, rows), pl.ds(start, columns)
            halves = head_halves(width, columns)
            masks = jnp.concatenate([key_mask[seen, :]] * len(halves), axis=0)
            keys = widened(apart(scaled(key[seen, lanes], width), halves), masks)
            half_score = dot_nt(widened(query[own, lanes], query_mask[own, :]), keys)
            if diagonal:
                half_score = causal(half_score, columns, first - start, True)
            weights = half_score + half_score * jnp.tanh(half_score)
            total[own, lanes] += dot(weights.astype(bf16), apart(value[seen, lanes], halves))

    each_group(model_width, step)


def query_pair(query, query_mask, grad, key, value, key_mask, total, width, diagonal):
    tokens, model_width = query.shape

    def step(lanes):
        for first, rows, start, columns in diagonal_spans(tokens, diagonal, True):
            own, seen = pl.ds(first, rows), pl.ds(start, columns)
            halves = head_halves(width, columns)
            masks = jnp.concatenate([key_mask[seen, :]] * len(halves), axis=0)
            plain_keys = apart(key[seen, lanes], halves)
            keys = widened(scaled(plain_keys, width), masks)
            half_score = dot_nt(widened(query[own, lanes], query_mask[own, :]), keys)
            if diagonal:
                half_score = causal(half_score, columns, first - start, True)
            grad_weights = dot_nt(
                grad[own, lanes], apart(scaled(value[seen, lanes], width), halves)
            )
            curve = 1.0 + jnp.tanh(half_score)
            slope = curve * (1.0 + half_score * (2.0 - curve))
            total[own, lanes] += dot((grad_weights * slope).astype(bf16), plain_keys)

    each_group(model_width, step)


def key_pair(
    query, query_mask, grad, key, value, key_mask, key_total, value_total, width, diagonal
):
    tokens, model_width = key.shape

    def step(lanes):
        for first, rows, start, columns in diagonal_spans(tokens, diagonal, False):
            own, seen = pl.ds(first, rows), pl.ds(start, columns)
            halves = head_halves(width, columns)
            masks = jnp.concatenate([query_mask[seen, :]] * len(halves), axis=0)
            plain_queries = apart(query[seen, lanes], halves)
            grads = apart(grad[seen, lanes], halves)
            half_score = dot_nt(
                widened(scaled(key[own, lanes], width), key_mask[own, :]),
                widened(plain_queries, masks),
            )
            if diagonal:
                half_score = causal(half_score, columns, first - start, False)
            grad_weights = dot_nt(scaled(value[own, lanes], width), grads)
            curve = 1.0 + jnp.tanh(half_score)
            weights = half_score * curve
            slope = curve + weights * (2.0 - curve)
            value_total[own, lanes] += dot(weights.astype(bf16), grads)
            key_total[own, lanes] += dot((grad_weights * slope).astype(bf16), plain_queries)

    each_group(model_width, step)


def project(rows, w_in, block):
    width = rows.shape[1]
    return silu(dot(rows[...], w_in[:, pl.ds(block * width, width)])).astype(bf16)


def near_kernel(
    width, place, seen, own, near, w_in, query_mask, key_mask, u_out, v_out, q_out, k_out, total,
    near_key, near_value,
):
    model_width = own.shape[1]
    me = place[0]
    for block, out in ((3, k_out), (1, v_out), (2, q_out), (0, u_out)):
        columns = pl.ds(block * model_width, model_width)
        out[...] = silu(dot(own[...], w_in[:, columns])).astype(bf16)
    total[...] = jnp.zeros_like(total)
    forward_pair(
        q_out, query_mask.at[me], k_out, v_out, key_mask.at[me], total, width, True
    )
    other = jnp.bitwise_xor(me, 1)

    @pl.when((other < me) & (seen[me, other] > 0))
    def _():
        value_columns = pl.ds(model_width, model_width)
        key_columns = pl.ds(3 * model_width, model_width)
        near_key[...] = silu(dot(near[...], w_in[:, key_columns])).astype(bf16)
        near_value[...] = silu(dot(near[...], w_in[:, value_columns])).astype(bf16)
        forward_pair(
            q_out, query_mask.at[me], near_key, near_value, key_mask.at[other], total, width, False
        )


def split_product(turned, right, half_bit, kept_out, sent_out, columns):
    half = turned.shape[0] // 2
    kept_rows = pl.ds(pl.multiple_of(half_bit * half, half), half)
    sent_rows = pl.ds(pl.multiple_of((1 - half_bit) * half, half), half)
    sent_out[:, columns] = dot(turned[sent_rows, :], right)
    kept_out[:, columns] = dot(turned[kept_rows, :], right)


def far_kernel(width, count, place, seen, *refs):
    far = refs[:count]
    (w_in, query, u_rows, query_mask, key_mask, near_total, out_grad, w_out, own, action, order) = (
        refs[count : count + 11]
    )
    (
        grad_attend_out, layer_out, gate_grad_pre, kept_out, sent_out, total, far_key, far_value,
        turned,
    ) = refs[count + 11 :]
    model_width = query.shape[1]
    me = place[0]
    total[...] = near_total[...]
    for index in range(count):
        other = jnp.bitwise_xor(me, index + 2)

        @pl.when((other < me) & (seen[me, other] > 0))
        def _():
            value_columns = pl.ds(model_width, model_width)
            key_columns = pl.ds(3 * model_width, model_width)
            rows = far[index]
            far_key[...] = silu(dot(rows[...], w_in[:, key_columns])).astype(bf16)
            far_value[...] = silu(dot(rows[...], w_in[:, value_columns])).astype(bf16)
            forward_pair(
                query, query_mask.at[me], far_key, far_value, key_mask.at[other], total, width,
                False,
            )

    attend_norm, attend_spread = normalize(total[...])
    unit_gate = u_rows[...].astype(f32)
    grad_gated = dot_nt(out_grad[...], w_out[...])
    grad_attend_out[...] = norm_back(grad_gated * unit_gate, attend_norm, attend_spread).astype(
        bf16
    )
    gated = (attend_norm * unit_gate).astype(bf16)
    layer_out[...] = (dot(gated, w_out[...]) + action[...].astype(f32)).astype(bf16)
    pre_act = dot(own[...], w_in[:, pl.ds(0, model_width)])
    grad_pre = (grad_gated * attend_norm * silu_slope(pre_act)).astype(bf16)
    gate_grad_pre[...] = grad_pre
    half_bit = jnp.bitwise_and(me, 1)
    turned[...] = dot_nt(order[...], gated).astype(bf16)
    split_product(turned, out_grad[...], half_bit, kept_out, sent_out, pl.ds(0, model_width))
    turned[...] = dot_nt(order[...], own[...]).astype(bf16)
    split_product(turned, grad_pre, half_bit, kept_out, sent_out, pl.ds(model_width, model_width))


def inner_kernel(
    width, arrive, place, seen, query, key, value, grad, query_mask, key_mask, w_in, near, near_grad,
    query_total, key_total, value_total, near_key, near_value,
):
    model_width = query.shape[1]
    me = place[0]
    other = jnp.bitwise_xor(me, 1)
    query_total[...] = jnp.zeros_like(query_total)
    key_total[...] = jnp.zeros_like(key_total)
    value_total[...] = jnp.zeros_like(value_total)
    query_pair(
        query, query_mask.at[me], grad, key, value, key_mask.at[me], query_total, width, True
    )
    key_pair(
        query, query_mask.at[me], grad, key, value, key_mask.at[me], key_total, value_total, width,
        True,
    )
    arrive()

    @pl.when((other < me) & (seen[me, other] > 0))
    def _():
        near_key[...] = project(near, w_in, 3)
        near_value[...] = project(near, w_in, 1)
        query_pair(
            query, query_mask.at[me], grad, near_key, near_value, key_mask.at[other], query_total,
            width, False,
        )

    @pl.when((other > me) & (seen[other, me] > 0))
    def _():
        near_key[...] = project(near, w_in, 2)
        key_pair(
            near_key, query_mask.at[other], near_grad, key, value, key_mask.at[me], key_total,
            value_total, width, False,
        )


def outer_kernel(
    width, count, arrive, place, seen, query, key, value, grad, query_mask, key_mask, w_in, query_grad,
    key_grad, value_grad, own, action, out_grad, gate_grad_pre, order, target, *refs
):
    rows = refs[:count]
    grads = refs[count : 2 * count]
    (
        sending, kept_out, sent_out, query_total, key_total, value_total, far_key, far_value, turned,
    ) = refs[2 * count :]
    model_width = key.shape[1]
    me = place[0]
    for total in (query_total, key_total, value_total):
        total[...] = jnp.zeros_like(total)
    for index in range(count):
        other = jnp.bitwise_xor(me, index + 2)

        @pl.when((other < me) & (seen[me, other] > 0))
        def _():
            far_key[...] = project(rows[index], w_in, 3)
            far_value[...] = project(rows[index], w_in, 1)
            query_pair(
                query, query_mask.at[me], grad, far_key, far_value, key_mask.at[other],
                query_total, width, False,
            )

        @pl.when((other > me) & (seen[other, me] > 0))
        def _():
            far_key[...] = project(rows[index], w_in, 2)
            key_pair(
                far_key, query_mask.at[other], grads[index], key, value, key_mask.at[me],
                key_total, value_total, width, False,
            )

    arrive()
    half_bit = jnp.bitwise_and(me, 1)
    turned[...] = dot_nt(order[...], own[...]).astype(bf16)
    grad_normed = dot_nt(gate_grad_pre[...], w_in[:, pl.ds(0, model_width)])
    for place_out, (block, near, far) in enumerate(
        ((1, value_grad, value_total), (2, query_grad, query_total), (3, key_grad, key_total))
    ):
        columns = pl.ds(block * model_width, model_width)
        pre_act = dot(own[...], w_in[:, columns])
        grad_pre = ((near[...] + far[...]) * silu_slope(pre_act)).astype(bf16)
        grad_normed += dot_nt(grad_pre, w_in[:, columns])
        split_product(
            turned, grad_pre, half_bit, kept_out, sent_out,
            pl.ds(place_out * model_width, model_width),
        )
    normed, spread = normalize(action[...].astype(f32))
    grad_action = norm_back(grad_normed, normed, spread) + out_grad[...].astype(f32)
    slot = lax.broadcasted_iota(jnp.int32, (sending.shape[0], key.shape[0]), 0)
    hits = jnp.where(slot == target[...], 1.0, 0.0).astype(bf16)
    sending[...] = dot(hits, grad_action.astype(bf16)).astype(bf16)


def call(
    kernel, name, scalars, arrays, outs, scratch=(), flops=0, vmem=VMEM_BYTES, late=()
):
    touched = sum(math.prod(a.shape) * a.dtype.itemsize for a in list(arrays) + list(outs))
    first = len(scalars)

    def run(*refs):
        end = len(refs) - len(late) - 1
        refs, buffers, semaphores = list(refs[:end]), refs[end:-1], refs[-1]
        copies = []
        for slot, (index, buffer) in enumerate(zip(late, buffers)):
            copies.append(
                pltpu.make_async_copy(refs[first + index], buffer, semaphores.at[slot])
            )
            copies[-1].start()
            refs[first + index] = buffer

        def arrive():
            for copy in copies:
                copy.wait()

        kernel(arrive, *refs)

    held = [pltpu.VMEM(arrays[index].shape, arrays[index].dtype) for index in late]
    spaces = [pl.ANY if index in late else pltpu.VMEM for index in range(len(arrays))]
    return pl.pallas_call(
        run if late else kernel,
        name=name,
        out_shape=tuple(outs),
        in_specs=[pl.BlockSpec(memory_space=pltpu.SMEM)] * len(scalars)
        + [pl.BlockSpec(memory_space=space) for space in spaces],
        out_specs=tuple([pl.BlockSpec(memory_space=pltpu.VMEM)] * len(outs)),
        scratch_shapes=list(scratch)
        + (held + [pltpu.SemaphoreType.DMA((len(late),))] if late else []),
        compiler_params=pltpu.CompilerParams(vmem_limit_bytes=vmem),
        cost_estimate=pl.CostEstimate(flops=flops, bytes_accessed=touched, transcendentals=0),
    )(*scalars, *arrays)


def shaped(shape, dtype):
    return jax.ShapeDtypeStruct(shape, dtype)


def bits_of(size):
    return (size - 1).bit_length()


def swap(values, axis, bit, useful=None):
    count = lax.axis_size(axis)
    pairs = [(i, i ^ (1 << bit)) for i in range(count)]
    if useful is not None:
        pairs = [pair for pair in pairs if useful(*pair)]
    return lax.ppermute(values, axis, pairs)


def spread_own(own, axis, upward_only):
    return spread_step({0: own}, [0], axis, upward_only)


def spread_step(held, offsets, axis, upward_only):
    held = dict(held)
    for bit in reversed(range(bits_of(lax.axis_size(axis)))):
        for offset in offsets:
            if offset & ((2 << bit) - 1) == 0 and offset ^ (1 << bit) not in held:
                keep = (lambda src, dst: (src ^ offset) > dst) if upward_only else None
                held[offset ^ (1 << bit)] = swap(held[offset], axis, bit, keep)
    return held


def spread_rest(held, axis, upward_only):
    while len(held) < lax.axis_size(axis):
        held = spread_step(held, sorted(set(held) - {0}), axis, upward_only)
    return [held[offset] for offset in range(1, lax.axis_size(axis))]


def after(values, witness):
    return lax.optimization_barrier((values, witness))[0]


def halving_steps():
    pair, dp = (
        [(axis, bit) for bit in range(bits_of(lax.axis_size(axis)))] for axis in ("pair", "dp")
    )
    return pair[:1] + dp[:1] + pair[1:] + dp[1:]


def order_matrix(model_width, shards, steps):
    pair_bits = bits_of(lax.axis_size("pair"))
    each = model_width // shards
    place = jnp.arange(model_width, dtype=jnp.int32)
    device = jnp.zeros_like(place)
    for depth, (axis, bit) in enumerate(steps):
        digit = (place // each >> (len(steps) - 1 - depth)) & 1
        device = device | (digit << (bit + (pair_bits if axis == "dp" else 0)))
    source = device * each + place % each
    return (source[:, None] == place[None, :]).astype(bf16)


class Halving:
    def __init__(self, kept, sent, steps, narrow):
        self.steps, self.narrow = steps, narrow
        self.kept, self.received = kept, swap(sent, *steps[0])

    def half(self, which):
        axis, bit = self.steps[1]
        size = self.kept.shape[0] // 2
        mine = (lax.axis_index(axis) >> bit) & 1
        start = (mine if which == "kept" else 1 - mine) * size
        return lax.dynamic_slice_in_dim(self.kept, start, size, 0) + lax.dynamic_slice_in_dim(
            self.received, start, size, 0
        ).astype(f32)

    def leaving(self):
        sent = self.half("sent")
        return sent.astype(bf16) if self.steps[1] in self.narrow else sent

    def step(self, sent=None):
        kept = self.half("kept")
        sent = self.leaving() if sent is None else sent
        return Halving(kept, sent, self.steps[1:], self.narrow)

    def total(self):
        return self.kept + self.received.astype(f32)


def body(table, accum, item_row, segments, pairs, w_in, w_out, out_grad):
    tokens = item_row.shape[0]
    rows_dev, model_width = table.shape
    shards = lax.axis_size(("dp", "pair"))
    span = lax.axis_size("pair")
    here = lax.axis_index("pair")
    bound_rows = 2 * (tokens // shards)
    width = model_width // HEADS
    factor = 1.0 / math.sqrt(tokens * shards)

    owner_ids = item_row // rows_dev
    row_slot = item_row % rows_dev
    shard_ids = jnp.arange(shards, dtype=jnp.int32)
    onehot = (owner_ids[:, None] == shard_ids[None, :]).astype(jnp.int32)
    bucket_rank = jnp.sum(jnp.cumsum(onehot, axis=0) * onehot, axis=1) - 1
    target = owner_ids * bound_rows + bucket_rank
    target_row = target.reshape(1, tokens)
    slots = jnp.arange(shards * bound_rows, dtype=jnp.int32)
    hits = slots[:, None] == target[None, :]
    request = jnp.sum(jnp.where(hits, row_slot[None, :], 0), axis=1).reshape(shards, bound_rows)
    slot_ids = lax.all_to_all(
        request, ("dp", "pair"), split_axis=0, concat_axis=0, tiled=True
    ).reshape(-1)
    table_places = jnp.arange(rows_dev, dtype=jnp.int32)
    found_rows = dot(
        (slot_ids[:, None] == table_places[None, :]).astype(bf16), table.astype(bf16)
    ).astype(bf16)
    fetched = lax.all_to_all(
        found_rows.reshape(shards, bound_rows, model_width),
        ("dp", "pair"), split_axis=0, concat_axis=0, tiled=True,
    ).reshape(shards * bound_rows, model_width)
    action = dot((target[:, None] == slots[None, :]).astype(bf16), fetched).astype(bf16)
    normed, _ = normalize(action.astype(f32))
    own, target_row = lax.optimization_barrier((normed.astype(bf16), target_row))

    blocks = jnp.arange(span, dtype=jnp.int32)
    pair_list = pairs[0]
    present = jnp.any(
        (pair_list[:, 0, None, None] == blocks[None, :, None])
        & (pair_list[:, 1, None, None] == blocks[None, None, :]),
        axis=0,
    )
    block_segments = segments[0].reshape(span, tokens)
    reaches = block_segments[:, -1][None, :] >= block_segments[:, 0][:, None]
    seen = (present & reaches).astype(jnp.int32)
    place = here.astype(jnp.int32).reshape(1)
    lane = jnp.arange(LANES, dtype=jnp.int32)[None, None, :]
    later = (block_segments == 1)[:, :, None]
    first_lane, second_lane = lane == 0, lane == 1
    key_mask = jnp.where(
        (first_lane & ~later) | (second_lane & later), FAR, 0.0
    ).astype(bf16)
    query_mask = jnp.where(
        (first_lane & later) | (second_lane & ~later), -1.0, 0.0
    ).astype(bf16)
    scalars = (place, seen)

    wide_f32 = shaped((tokens, model_width), f32)
    wide_bf16 = shaped((tokens, model_width), bf16)
    scratch_f32 = pltpu.VMEM((tokens, model_width), f32)
    scratch_bf16 = pltpu.VMEM((tokens, model_width), bf16)
    pair_flops = 2 * tokens * tokens * model_width * 4

    held = spread_own(own, "pair", False)
    count = span - 1
    u_rows, value, query, key, near_total = call(
        functools.partial(near_kernel, width), "near_attention", scalars,
        (own, held[1], w_in, query_mask, key_mask),
        (wide_bf16, wide_bf16, wide_bf16, wide_bf16, wide_f32),
        (scratch_bf16, scratch_bf16),
        flops=4 * pair_flops,
    )
    held = {0: own, 1: held[1], **after({k: v for k, v in held.items() if k > 1}, near_total)}
    rows = spread_rest(held, "pair", False)
    steps = halving_steps()
    order = order_matrix(model_width, shards, steps)
    half_width = model_width // 2
    scratch_turned = pltpu.VMEM((model_width, tokens), bf16)
    early_part = shaped((half_width, 2 * model_width), f32)
    late_part = shaped((half_width, 3 * model_width), f32)
    grad_attend, layer_out, gate_grad_pre, early_kept, early_sent = call(
        functools.partial(far_kernel, width, count - 1), "far_attention", scalars,
        (
            *rows[1:], w_in, query, u_rows, query_mask, key_mask, near_total, out_grad, w_out, own,
            action, order,
        ),
        (wide_bf16, wide_bf16, wide_bf16, early_part, early_part),
        (scratch_f32, scratch_bf16, scratch_bf16, scratch_turned),
        flops=4 * pair_flops,
    )
    held = spread_own(grad_attend, "pair", True)
    early = Halving(early_kept, early_sent, steps, (steps[1], steps[-2]))
    early_leaving, grad_attend = lax.optimization_barrier((early.leaving(), grad_attend))
    early = early.step(early_leaving)
    query_grad, key_grad, value_grad = call(
        functools.partial(inner_kernel, width), "near_gradients", scalars,
        (query, key, value, grad_attend, query_mask, key_mask, w_in, rows[0], held[1]),
        (wide_f32, wide_f32, wide_f32),
        (scratch_bf16, scratch_bf16),
        flops=12 * pair_flops,
        late=(6, 7, 8),
        vmem=3 * VMEM_BYTES,
    )
    early.received = after(early.received, query_grad)
    early_leaving, others = lax.optimization_barrier(
        (early.leaving(), {k: v for k, v in held.items() if k > 0})
    )
    early = early.step(early_leaving)
    grads = spread_rest({0: grad_attend, **others}, "pair", True)
    sending, late_kept, late_sent = call(
        functools.partial(outer_kernel, width, count - 1), "far_gradients", scalars,
        (
            query, key, value, grad_attend, query_mask, key_mask, w_in, query_grad, key_grad,
            value_grad, own, action, out_grad, gate_grad_pre, order, target_row, *rows[1:],
            *grads[1:],
        ),
        (shaped((shards * bound_rows, model_width), bf16), late_part, late_part),
        (scratch_f32, scratch_f32, scratch_f32, scratch_bf16, scratch_bf16, scratch_turned),
        flops=12 * pair_flops,
        late=tuple(range(7, 15)),
        vmem=3 * VMEM_BYTES,
    )
    early.received, sending, late_kept, late_sent = lax.optimization_barrier(
        (early.received, sending, late_kept, late_sent)
    )
    late = Halving(late_kept, late_sent, steps, steps[1:3])
    returned = lax.all_to_all(
        sending.reshape(shards, bound_rows, model_width),
        ("dp", "pair"), split_axis=0, concat_axis=0, tiled=True,
    ).reshape(shards * bound_rows, model_width)
    late = late.step()
    late_leaving, returned = lax.optimization_barrier((late.leaving(), returned))
    late = late.step(late_leaving)
    early.received = after(early.received, late.kept)
    while len(late.steps) > 1:
        late = late.step()
    while len(early.steps) > 1:
        early = early.step()
    first, late = early.total(), late.total()
    grad_out = first[:, :model_width] * factor
    grad_in = factor * jnp.concatenate([first[:, model_width:], late], axis=1)
    row_total = dot((table_places[:, None] == slot_ids[None, :]).astype(bf16), returned)
    accum_new = accum + jnp.mean(row_total * row_total, axis=1)
    table_new = table - learn_rate * row_total / jnp.sqrt(accum_new)[:, None]
    return (layer_out, table_new, accum_new, grad_in, grad_out)


def solution(mesh):
    placed = (
        P(("dp", "pair"), None),
        P(("dp", "pair")),
        P(("dp", "pair")),
        P("dp", None),
        P("dp", None, None),
        P(),
        P(),
        P(("dp", "pair"), None),
    )
    return jax.shard_map(
        body,
        mesh=mesh,
        in_specs=placed,
        out_specs=(
            P(("dp", "pair"), None),
            P(("dp", "pair"), None),
            P(("dp", "pair")),
            P(("dp", "pair"), None),
            P(("dp", "pair"), None),
        ),
        check_vma=False,
    )
```

```python
import functools
import math

import jax
import jax.numpy as jnp
from jax import lax
from jax.experimental import pallas as pl
from jax.experimental.pallas import tpu as pltpu
from jax.sharding import PartitionSpec as P

HEADS = 8
LANES = 128
UNROLL = 4
FAR = float(2**30)
VMEM_BYTES = 20 * 1024 * 1024

norm_eps = 1e-05
learn_rate = 0.5
f32 = jnp.float32
bf16 = jnp.bfloat16


def dot(left, right):
    return lax.dot_general(left, right, (((1,), (0,)), ((), ())), preferred_element_type=f32)


def dot_nt(left, right):
    return lax.dot_general(left, right, (((1,), (1,)), ((), ())), preferred_element_type=f32)


def normalize(values):
    row_mean = jnp.mean(values, axis=-1, keepdims=True)
    centred = values - row_mean
    spread = jnp.sqrt(jnp.mean(centred * centred, axis=-1, keepdims=True) + norm_eps)
    return (centred / spread, spread)


def norm_back(grad_rows, normed, spread):
    first_mean = jnp.mean(grad_rows, axis=-1, keepdims=True)
    second_mean = jnp.mean(grad_rows * normed, axis=-1, keepdims=True)
    return (grad_rows - first_mean - normed * second_mean) / spread


def silu(values):
    half = 0.5 * values
    return half + half * jnp.tanh(half)


def silu_slope(values):
    half = 0.5 * values
    curve = jnp.tanh(half)
    return (0.5 + 0.5 * curve) * (1.0 + half * (1.0 - curve))


def head_halves(width, rows):
    lane = lax.broadcasted_iota(jnp.int32, (rows, LANES), 1)
    return [(lane >= start) & (lane < start + width) for start in range(0, LANES, width)]


def causal(scores, columns, lead, lower):
    row = lax.broadcasted_iota(jnp.int32, scores.shape, 0) + lead
    column = lax.broadcasted_iota(jnp.int32, scores.shape, 1) % columns
    return jnp.where(column <= row if lower else row <= column, scores, -FAR)


def apart(rows, halves):
    nothing = jnp.zeros_like(rows)
    return jnp.concatenate([jnp.where(half, rows, nothing) for half in halves], axis=0)


def widened(rows, mask):
    return jnp.concatenate([rows, mask], axis=1)


def scaled(rows, width):
    return rows * jnp.asarray(0.5 / math.sqrt(width), bf16)


def each_group(model_width, step):
    def one(group, carry):
        step(pl.ds(pl.multiple_of(group * LANES, LANES), LANES))
        return carry

    lax.fori_loop(0, model_width // LANES, one, 0, unroll=UNROLL)


def diagonal_spans(tokens, diagonal, lower):
    if not diagonal:
        return [(0, tokens, 0, tokens)]
    cut = tokens - LANES if lower else LANES
    if lower:
        return [(0, cut, 0, cut), (cut, tokens - cut, 0, tokens)]
    return [(0, cut, 0, tokens), (cut, tokens - cut, cut, tokens - cut)]


def forward_pair(query, query_mask, key, value, key_mask, total, width, diagonal):
    tokens, model_width = query.shape

    def step(lanes):
        for first, rows, start, columns in diagonal_spans(tokens, diagonal, True):
            own, seen = pl.ds(first, rows), pl.ds(start, columns)
            halves = head_halves(width, columns)
            masks = jnp.concatenate([key_mask[seen, :]] * len(halves), axis=0)
            keys = widened(apart(scaled(key[seen, lanes], width), halves), masks)
            half_score = dot_nt(widened(query[own, lanes], query_mask[own, :]), keys)
            if diagonal:
                half_score = causal(half_score, columns, first - start, True)
            weights = half_score + half_score * jnp.tanh(half_score)
            total[own, lanes] += dot(weights.astype(bf16), apart(value[seen, lanes], halves))

    each_group(model_width, step)


def query_pair(query, query_mask, grad, key, value, key_mask, total, width, diagonal):
    tokens, model_width = query.shape

    def step(lanes):
        for first, rows, start, columns in diagonal_spans(tokens, diagonal, True):
            own, seen = pl.ds(first, rows), pl.ds(start, columns)
            halves = head_halves(width, columns)
            masks = jnp.concatenate([key_mask[seen, :]] * len(halves), axis=0)
            plain_keys = apart(key[seen, lanes], halves)
            keys = widened(scaled(plain_keys, width), masks)
            half_score = dot_nt(widened(query[own, lanes], query_mask[own, :]), keys)
            if diagonal:
                half_score = causal(half_score, columns, first - start, True)
            grad_weights = dot_nt(
                grad[own, lanes], apart(scaled(value[seen, lanes], width), halves)
            )
            curve = 1.0 + jnp.tanh(half_score)
            slope = curve * (1.0 + half_score * (2.0 - curve))
            total[own, lanes] += dot((grad_weights * slope).astype(bf16), plain_keys)

    each_group(model_width, step)


def key_pair(
    query, query_mask, grad, key, value, key_mask, key_total, value_total, width, diagonal
):
    tokens, model_width = key.shape

    def step(lanes):
        for first, rows, start, columns in diagonal_spans(tokens, diagonal, False):
            own, seen = pl.ds(first, rows), pl.ds(start, columns)
            halves = head_halves(width, columns)
            masks = jnp.concatenate([query_mask[seen, :]] * len(halves), axis=0)
            plain_queries = apart(query[seen, lanes], halves)
            grads = apart(grad[seen, lanes], halves)
            half_score = dot_nt(
                widened(scaled(key[own, lanes], width), key_mask[own, :]),
                widened(plain_queries, masks),
            )
            if diagonal:
                half_score = causal(half_score, columns, first - start, False)
            grad_weights = dot_nt(scaled(value[own, lanes], width), grads)
            curve = 1.0 + jnp.tanh(half_score)
            weights = half_score * curve
            slope = curve + weights * (2.0 - curve)
            value_total[own, lanes] += dot(weights.astype(bf16), grads)
            key_total[own, lanes] += dot((grad_weights * slope).astype(bf16), plain_queries)

    each_group(model_width, step)


def project(rows, w_in, block):
    width = rows.shape[1]
    return silu(dot(rows[...], w_in[:, pl.ds(block * width, width)])).astype(bf16)


def near_kernel(
    width, place, seen, own, near, w_in, query_mask, key_mask, u_out, v_out, q_out, k_out, total,
    near_key, near_value,
):
    model_width = own.shape[1]
    me = place[0]
    for block, out in ((3, k_out), (1, v_out), (2, q_out), (0, u_out)):
        columns = pl.ds(block * model_width, model_width)
        out[...] = silu(dot(own[...], w_in[:, columns])).astype(bf16)
    total[...] = jnp.zeros_like(total)
    forward_pair(
        q_out, query_mask.at[me], k_out, v_out, key_mask.at[me], total, width, True
    )
    other = jnp.bitwise_xor(me, 1)

    @pl.when((other < me) & (seen[me, other] > 0))
    def _():
        value_columns = pl.ds(model_width, model_width)
        key_columns = pl.ds(3 * model_width, model_width)
        near_key[...] = silu(dot(near[...], w_in[:, key_columns])).astype(bf16)
        near_value[...] = silu(dot(near[...], w_in[:, value_columns])).astype(bf16)
        forward_pair(
            q_out, query_mask.at[me], near_key, near_value, key_mask.at[other], total, width, False
        )


def split_product(turned, right, half_bit, kept_out, sent_out, columns):
    half = turned.shape[0] // 2
    kept_rows = pl.ds(pl.multiple_of(half_bit * half, half), half)
    sent_rows = pl.ds(pl.multiple_of((1 - half_bit) * half, half), half)
    sent_out[:, columns] = dot(turned[sent_rows, :], right)
    kept_out[:, columns] = dot(turned[kept_rows, :], right)


def far_kernel(width, count, place, seen, *refs):
    far = refs[:count]
    (w_in, query, u_rows, query_mask, key_mask, near_total, out_grad, w_out, own, action, order) = (
        refs[count : count + 11]
    )
    (
        grad_attend_out, layer_out, gate_grad_pre, kept_out, sent_out, total, far_key, far_value,
        turned,
    ) = refs[count + 11 :]
    model_width = query.shape[1]
    me = place[0]
    total[...] = near_total[...]
    for index in range(count):
        other = jnp.bitwise_xor(me, index + 2)

        @pl.when((other < me) & (seen[me, other] > 0))
        def _():
            value_columns = pl.ds(model_width, model_width)
            key_columns = pl.ds(3 * model_width, model_width)
            rows = far[index]
            far_key[...] = silu(dot(rows[...], w_in[:, key_columns])).astype(bf16)
            far_value[...] = silu(dot(rows[...], w_in[:, value_columns])).astype(bf16)
            forward_pair(
                query, query_mask.at[me], far_key, far_value, key_mask.at[other], total, width,
                False,
            )

    attend_norm, attend_spread = normalize(total[...])
    unit_gate = u_rows[...].astype(f32)
    grad_gated = dot_nt(out_grad[...], w_out[...])
    grad_attend_out[...] = norm_back(grad_gated * unit_gate, attend_norm, attend_spread).astype(
        bf16
    )
    gated = (attend_norm * unit_gate).astype(bf16)
    layer_out[...] = (dot(gated, w_out[...]) + action[...].astype(f32)).astype(bf16)
    pre_act = dot(own[...], w_in[:, pl.ds(0, model_width)])
    grad_pre = (grad_gated * attend_norm * silu_slope(pre_act)).astype(bf16)
    gate_grad_pre[...] = grad_pre
    half_bit = jnp.bitwise_and(me, 1)
    turned[...] = dot_nt(order[...], gated).astype(bf16)
    split_product(turned, out_grad[...], half_bit, kept_out, sent_out, pl.ds(0, model_width))
    turned[...] = dot_nt(order[...], own[...]).astype(bf16)
    split_product(turned, grad_pre, half_bit, kept_out, sent_out, pl.ds(model_width, model_width))


def inner_kernel(
    width, arrive, place, seen, query, key, value, grad, query_mask, key_mask, w_in, near, near_grad,
    query_total, key_total, value_total, near_key, near_value,
):
    model_width = query.shape[1]
    me = place[0]
    other = jnp.bitwise_xor(me, 1)
    query_total[...] = jnp.zeros_like(query_total)
    key_total[...] = jnp.zeros_like(key_total)
    value_total[...] = jnp.zeros_like(value_total)
    query_pair(
        query, query_mask.at[me], grad, key, value, key_mask.at[me], query_total, width, True
    )
    key_pair(
        query, query_mask.at[me], grad, key, value, key_mask.at[me], key_total, value_total, width,
        True,
    )
    arrive()

    @pl.when((other < me) & (seen[me, other] > 0))
    def _():
        near_key[...] = project(near, w_in, 3)
        near_value[...] = project(near, w_in, 1)
        query_pair(
            query, query_mask.at[me], grad, near_key, near_value, key_mask.at[other], query_total,
            width, False,
        )

    @pl.when((other > me) & (seen[other, me] > 0))
    def _():
        near_key[...] = project(near, w_in, 2)
        key_pair(
            near_key, query_mask.at[other], near_grad, key, value, key_mask.at[me], key_total,
            value_total, width, False,
        )


def outer_kernel(
    width, count, arrive, place, seen, query, key, value, grad, query_mask, key_mask, w_in, query_grad,
    key_grad, value_grad, own, action, out_grad, gate_grad_pre, order, target, *refs
):
    rows = refs[:count]
    grads = refs[count : 2 * count]
    (
        sending, kept_out, sent_out, query_total, key_total, value_total, far_key, far_value, turned,
    ) = refs[2 * count :]
    model_width = key.shape[1]
    me = place[0]
    for total in (query_total, key_total, value_total):
        total[...] = jnp.zeros_like(total)
    for index in range(count):
        other = jnp.bitwise_xor(me, index + 2)

        @pl.when((other < me) & (seen[me, other] > 0))
        def _():
            far_key[...] = project(rows[index], w_in, 3)
            far_value[...] = project(rows[index], w_in, 1)
            query_pair(
                query, query_mask.at[me], grad, far_key, far_value, key_mask.at[other],
                query_total, width, False,
            )

        @pl.when((other > me) & (seen[other, me] > 0))
        def _():
            far_key[...] = project(rows[index], w_in, 2)
            key_pair(
                far_key, query_mask.at[other], grads[index], key, value, key_mask.at[me],
                key_total, value_total, width, False,
            )

    arrive()
    half_bit = jnp.bitwise_and(me, 1)
    turned[...] = dot_nt(order[...], own[...]).astype(bf16)
    grad_normed = dot_nt(gate_grad_pre[...], w_in[:, pl.ds(0, model_width)])
    for place_out, (block, near, far) in enumerate(
        ((1, value_grad, value_total), (2, query_grad, query_total), (3, key_grad, key_total))
    ):
        columns = pl.ds(block * model_width, model_width)
        pre_act = dot(own[...], w_in[:, columns])
        grad_pre = ((near[...] + far[...]) * silu_slope(pre_act)).astype(bf16)
        grad_normed += dot_nt(grad_pre, w_in[:, columns])
        split_product(
            turned, grad_pre, half_bit, kept_out, sent_out,
            pl.ds(place_out * model_width, model_width),
        )
    normed, spread = normalize(action[...].astype(f32))
    grad_action = norm_back(grad_normed, normed, spread) + out_grad[...].astype(f32)
    slot = lax.broadcasted_iota(jnp.int32, (sending.shape[0], key.shape[0]), 0)
    hits = jnp.where(slot == target[...], 1.0, 0.0).astype(bf16)
    sending[...] = dot(hits, grad_action.astype(bf16)).astype(bf16)


def call(
    kernel, name, scalars, arrays, outs, scratch=(), flops=0, vmem=VMEM_BYTES, late=()
):
    touched = sum(math.prod(a.shape) * a.dtype.itemsize for a in list(arrays) + list(outs))
    first = len(scalars)

    def run(*refs):
        end = len(refs) - len(late) - 1
        refs, buffers, semaphores = list(refs[:end]), refs[end:-1], refs[-1]
        copies = []
        for slot, (index, buffer) in enumerate(zip(late, buffers)):
            copies.append(
                pltpu.make_async_copy(refs[first + index], buffer, semaphores.at[slot])
            )
            copies[-1].start()
            refs[first + index] = buffer

        def arrive():
            for copy in copies:
                copy.wait()

        kernel(arrive, *refs)

    held = [pltpu.VMEM(arrays[index].shape, arrays[index].dtype) for index in late]
    spaces = [pl.ANY if index in late else pltpu.VMEM for index in range(len(arrays))]
    return pl.pallas_call(
        run if late else kernel,
        name=name,
        out_shape=tuple(outs),
        in_specs=[pl.BlockSpec(memory_space=pltpu.SMEM)] * len(scalars)
        + [pl.BlockSpec(memory_space=space) for space in spaces],
        out_specs=tuple([pl.BlockSpec(memory_space=pltpu.VMEM)] * len(outs)),
        scratch_shapes=list(scratch)
        + (held + [pltpu.SemaphoreType.DMA((len(late),))] if late else []),
        compiler_params=pltpu.CompilerParams(vmem_limit_bytes=vmem),
        cost_estimate=pl.CostEstimate(flops=flops, bytes_accessed=touched, transcendentals=0),
    )(*scalars, *arrays)


def shaped(shape, dtype):
    return jax.ShapeDtypeStruct(shape, dtype)


def bits_of(size):
    return (size - 1).bit_length()


def swap(values, axis, bit, useful=None):
    count = lax.axis_size(axis)
    pairs = [(i, i ^ (1 << bit)) for i in range(count)]
    if useful is not None:
        pairs = [pair for pair in pairs if useful(*pair)]
    return lax.ppermute(values, axis, pairs)


def spread_own(own, axis, upward_only):
    return spread_step({0: own}, [0], axis, upward_only)


def spread_step(held, offsets, axis, upward_only):
    held = dict(held)
    for bit in reversed(range(bits_of(lax.axis_size(axis)))):
        for offset in offsets:
            if offset & ((2 << bit) - 1) == 0 and offset ^ (1 << bit) not in held:
                keep = (lambda src, dst: (src ^ offset) > dst) if upward_only else None
                held[offset ^ (1 << bit)] = swap(held[offset], axis, bit, keep)
    return held


def spread_rest(held, axis, upward_only):
    while len(held) < lax.axis_size(axis):
        held = spread_step(held, sorted(set(held) - {0}), axis, upward_only)
    return [held[offset] for offset in range(1, lax.axis_size(axis))]


def after(values, witness):
    return lax.optimization_barrier((values, witness))[0]


def halving_steps():
    pair, dp = (
        [(axis, bit) for bit in range(bits_of(lax.axis_size(axis)))] for axis in ("pair", "dp")
    )
    return pair[:1] + dp[:1] + pair[1:] + dp[1:]


def order_matrix(model_width, shards, steps):
    pair_bits = bits_of(lax.axis_size("pair"))
    each = model_width // shards
    place = jnp.arange(model_width, dtype=jnp.int32)
    device = jnp.zeros_like(place)
    for depth, (axis, bit) in enumerate(steps):
        digit = (place // each >> (len(steps) - 1 - depth)) & 1
        device = device | (digit << (bit + (pair_bits if axis == "dp" else 0)))
    source = device * each + place % each
    return (source[:, None] == place[None, :]).astype(bf16)


class Halving:
    def __init__(self, kept, sent, steps, narrow):
        self.steps, self.narrow = steps, narrow
        self.kept, self.received = kept, swap(sent, *steps[0])

    def half(self, which):
        axis, bit = self.steps[1]
        size = self.kept.shape[0] // 2
        mine = (lax.axis_index(axis) >> bit) & 1
        start = (mine if which == "kept" else 1 - mine) * size
        return lax.dynamic_slice_in_dim(self.kept, start, size, 0) + lax.dynamic_slice_in_dim(
            self.received, start, size, 0
        ).astype(f32)

    def leaving(self):
        sent = self.half("sent")
        return sent.astype(bf16) if self.steps[1] in self.narrow else sent

    def step(self, sent=None):
        kept = self.half("kept")
        sent = self.leaving() if sent is None else sent
        return Halving(kept, sent, self.steps[1:], self.narrow)

    def total(self):
        return self.kept + self.received.astype(f32)


def body(table, accum, item_row, segments, pairs, w_in, w_out, out_grad):
    tokens = item_row.shape[0]
    rows_dev, model_width = table.shape
    shards = lax.axis_size(("dp", "pair"))
    span = lax.axis_size("pair")
    here = lax.axis_index("pair")
    bound_rows = 2 * (tokens // shards)
    width = model_width // HEADS
    factor = 1.0 / math.sqrt(tokens * shards)

    owner_ids = item_row // rows_dev
    row_slot = item_row % rows_dev
    shard_ids = jnp.arange(shards, dtype=jnp.int32)
    onehot = (owner_ids[:, None] == shard_ids[None, :]).astype(jnp.int32)
    bucket_rank = jnp.sum(jnp.cumsum(onehot, axis=0) * onehot, axis=1) - 1
    target = owner_ids * bound_rows + bucket_rank
    target_row = target.reshape(1, tokens)
    slots = jnp.arange(shards * bound_rows, dtype=jnp.int32)
    hits = slots[:, None] == target[None, :]
    request = jnp.sum(jnp.where(hits, row_slot[None, :], 0), axis=1).reshape(shards, bound_rows)
    slot_ids = lax.all_to_all(
        request, ("dp", "pair"), split_axis=0, concat_axis=0, tiled=True
    ).reshape(-1)
    table_places = jnp.arange(rows_dev, dtype=jnp.int32)
    found_rows = dot(
        (slot_ids[:, None] == table_places[None, :]).astype(bf16), table.astype(bf16)
    ).astype(bf16)
    fetched = lax.all_to_all(
        found_rows.reshape(shards, bound_rows, model_width),
        ("dp", "pair"), split_axis=0, concat_axis=0, tiled=True,
    ).reshape(shards * bound_rows, model_width)
    action = dot((target[:, None] == slots[None, :]).astype(bf16), fetched).astype(bf16)
    normed, _ = normalize(action.astype(f32))
    own, target_row = lax.optimization_barrier((normed.astype(bf16), target_row))

    blocks = jnp.arange(span, dtype=jnp.int32)
    pair_list = pairs[0]
    present = jnp.any(
        (pair_list[:, 0, None, None] == blocks[None, :, None])
        & (pair_list[:, 1, None, None] == blocks[None, None, :]),
        axis=0,
    )
    block_segments = segments[0].reshape(span, tokens)
    reaches = block_segments[:, -1][None, :] >= block_segments[:, 0][:, None]
    seen = (present & reaches).astype(jnp.int32)
    place = here.astype(jnp.int32).reshape(1)
    lane = jnp.arange(LANES, dtype=jnp.int32)[None, None, :]
    later = (block_segments == 1)[:, :, None]
    first_lane, second_lane = lane == 0, lane == 1
    key_mask = jnp.where(
        (first_lane & ~later) | (second_lane & later), FAR, 0.0
    ).astype(bf16)
    query_mask = jnp.where(
        (first_lane & later) | (second_lane & ~later), -1.0, 0.0
    ).astype(bf16)
    scalars = (place, seen)

    wide_f32 = shaped((tokens, model_width), f32)
    wide_bf16 = shaped((tokens, model_width), bf16)
    scratch_f32 = pltpu.VMEM((tokens, model_width), f32)
    scratch_bf16 = pltpu.VMEM((tokens, model_width), bf16)
    pair_flops = 2 * tokens * tokens * model_width * 4

    held = spread_own(own, "pair", False)
    count = span - 1
    u_rows, value, query, key, near_total = call(
        functools.partial(near_kernel, width), "near_attention", scalars,
        (own, held[1], w_in, query_mask, key_mask),
        (wide_bf16, wide_bf16, wide_bf16, wide_bf16, wide_f32),
        (scratch_bf16, scratch_bf16),
        flops=4 * pair_flops,
    )
    held = {0: own, 1: held[1], **after({k: v for k, v in held.items() if k > 1}, near_total)}
    rows = spread_rest(held, "pair", False)
    steps = halving_steps()
    order = order_matrix(model_width, shards, steps)
    half_width = model_width // 2
    scratch_turned = pltpu.VMEM((model_width, tokens), bf16)
    early_part = shaped((half_width, 2 * model_width), f32)
    late_part = shaped((half_width, 3 * model_width), f32)
    grad_attend, layer_out, gate_grad_pre, early_kept, early_sent = call(
        functools.partial(far_kernel, width, count - 1), "far_attention", scalars,
        (
            *rows[1:], w_in, query, u_rows, query_mask, key_mask, near_total, out_grad, w_out, own,
            action, order,
        ),
        (wide_bf16, wide_bf16, wide_bf16, early_part, early_part),
        (scratch_f32, scratch_bf16, scratch_bf16, scratch_turned),
        flops=4 * pair_flops,
    )
    held = spread_own(grad_attend, "pair", True)
    early = Halving(early_kept, early_sent, steps, (steps[1], steps[-2]))
    early_leaving, grad_attend = lax.optimization_barrier((early.leaving(), grad_attend))
    early = early.step(early_leaving)
    query_grad, key_grad, value_grad = call(
        functools.partial(inner_kernel, width), "near_gradients", scalars,
        (query, key, value, grad_attend, query_mask, key_mask, w_in, rows[0], held[1]),
        (wide_f32, wide_f32, wide_f32),
        (scratch_bf16, scratch_bf16),
        flops=12 * pair_flops,
        late=(6, 7, 8),
        vmem=VMEM_BYTES,
    )
    early.received = after(early.received, query_grad)
    early_leaving, others = lax.optimization_barrier(
        (early.leaving(), {k: v for k, v in held.items() if k > 0})
    )
    early = early.step(early_leaving)
    grads = spread_rest({0: grad_attend, **others}, "pair", True)
    sending, late_kept, late_sent = call(
        functools.partial(outer_kernel, width, count - 1), "far_gradients", scalars,
        (
            query, key, value, grad_attend, query_mask, key_mask, w_in, query_grad, key_grad,
            value_grad, own, action, out_grad, gate_grad_pre, order, target_row, *rows[1:],
            *grads[1:],
        ),
        (shaped((shards * bound_rows, model_width), bf16), late_part, late_part),
        (scratch_f32, scratch_f32, scratch_f32, scratch_bf16, scratch_bf16, scratch_turned),
        flops=12 * pair_flops,
        late=tuple(range(7, 15)),
        vmem=2 * VMEM_BYTES,
    )
    early.received, sending, late_kept, late_sent = lax.optimization_barrier(
        (early.received, sending, late_kept, late_sent)
    )
    late = Halving(late_kept, late_sent, steps, steps[1:3])
    returned = lax.all_to_all(
        sending.reshape(shards, bound_rows, model_width),
        ("dp", "pair"), split_axis=0, concat_axis=0, tiled=True,
    ).reshape(shards * bound_rows, model_width)
    late = late.step()
    late_leaving, returned = lax.optimization_barrier((late.leaving(), returned))
    late = late.step(late_leaving)
    early.received = after(early.received, late.kept)
    while len(late.steps) > 1:
        late = late.step()
    while len(early.steps) > 1:
        early = early.step()
    first, late = early.total(), late.total()
    grad_out = first[:, :model_width] * factor
    grad_in = factor * jnp.concatenate([first[:, model_width:], late], axis=1)
    row_total = dot((table_places[:, None] == slot_ids[None, :]).astype(bf16), returned)
    accum_new = accum + jnp.mean(row_total * row_total, axis=1)
    table_new = table - learn_rate * row_total / jnp.sqrt(accum_new)[:, None]
    return (layer_out, table_new, accum_new, grad_in, grad_out)


def solution(mesh):
    placed = (
        P(("dp", "pair"), None),
        P(("dp", "pair")),
        P(("dp", "pair")),
        P("dp", None),
        P("dp", None, None),
        P(),
        P(),
        P(("dp", "pair"), None),
    )
    return jax.shard_map(
        body,
        mesh=mesh,
        in_specs=placed,
        out_specs=(
            P(("dp", "pair"), None),
            P(("dp", "pair"), None),
            P(("dp", "pair")),
            P(("dp", "pair"), None),
            P(("dp", "pair"), None),
        ),
        check_vma=False,
    )
```
